128 devices in a mesh: gx: 8 (over y, core), gy: 16 (over x, z).
Axes of the slice: x: 4, y: 4, z: 4, core: 2. Of those that a mesh axis runs over, the one named last changes fastest.
Arguments:
- right_side: float32 [192, 1024, 512], P('gx', 'gy'), may hold values from -10 to 10
- alpha: float32 [192, 1024, 512], P('gx', 'gy'), may hold values from 0.1 to 1
- beta_x: float32 [192, 1024, 512], P('gx', 'gy'), may hold values from 0.1 to 1
- beta_y: float32 [192, 1024, 512], P('gx', 'gy'), may hold values from 0.1 to 1
- beta_z: float32 [192, 1024, 512], P('gx', 'gy'), may hold values from 0.1 to 1
Outputs:
- correction_fine: float32 [192, 1024, 512], P('gx', 'gy')
- correction_mid: float32 [96, 512, 256], P('gx', 'gy')
- correction_low: float32 [48, 256, 128], P('gx', 'gy')
- correction_top: float32 [24, 128, 64], P('gx', 'gy')
The draws below stay inside these ranges and needn't reach their ends.
All inputs are finite; a program needn't handle non-finite values.
Results may differ from the reference program's by a relative error of at most 0.0003.
Values sent between devices are 32-bit elements; how exact they have to be, the bound alone decides.
A program may use at most 192 MiB of HBM per device.

```python
import math
import jax
import jax.numpy as jnp

NZ = 512
DEGREE = 4
NX = 192
NY = 1024


def draw_right_side(key, part):
    key = jax.random.fold_in(key, 7)
    rough_key, phase_key = jax.random.split(key)
    rough = jnp.clip(jax.random.normal(rough_key, (NX, NY, NZ), jnp.float32), -6.0, 6.0)
    height = 2.0
    phases = jax.random.uniform(phase_key, (3,), jnp.float32, 0.0, 2.0 * math.pi)
    along_x = jnp.cos(2.0 * math.pi * jnp.arange(NX, dtype=jnp.float32) / NX + phases[0])
    along_y = jnp.cos(2.0 * math.pi * jnp.arange(NY, dtype=jnp.float32) / NY + phases[1])
    along_z = jnp.cos(2.0 * math.pi * jnp.arange(NZ, dtype=jnp.float32) / NZ + phases[2])
    smooth = height * along_x[:, None, None] * along_y[None, :, None] * along_z[None, None, :]
    return rough + smooth


def shard_levels(own_key, extent, cuts, least, top_value):
    loudness = 1.0
    for axis_at, parts in cuts:
        steps = jax.random.uniform(jax.random.fold_in(jax.random.fold_in(own_key, 6), axis_at), (parts,), jnp.float32, least / len(cuts), top_value / len(cuts))
        loudness = loudness * jnp.repeat(jnp.exp(steps), extent[axis_at] // parts).reshape((-1,) + (1,) * (len(extent) - 1 - axis_at))
    return loudness


def setup_inputs(seed: int = 0) -> dict:
    arg_keys = jax.random.split(jax.random.key(seed), 6)
    right_side = draw_right_side(jax.random.fold_in(arg_keys[5], 71), 0)
    alpha = jnp.clip(jnp.exp(math.log(1.0) - 2.3025851 * jax.random.uniform(arg_keys[1], (NX, NY, NZ), jnp.float32) ** shard_levels(arg_keys[1], (NX, NY, NZ), ((0, 8), (1, 16)), -0.2, 0.2)), 0.1, 1.0)
    beta_x = jnp.clip(jnp.exp(math.log(1.0) - 2.3025851 * jax.random.uniform(arg_keys[2], (NX, NY, NZ), jnp.float32) ** shard_levels(arg_keys[2], (NX, NY, NZ), ((0, 8), (1, 16)), -0.2, 0.2)), 0.1, 1.0)
    beta_y = jnp.clip(jnp.exp(math.log(1.0) - 2.3025851 * jax.random.uniform(arg_keys[3], (NX, NY, NZ), jnp.float32) ** shard_levels(arg_keys[3], (NX, NY, NZ), ((0, 8), (1, 16)), -0.2, 0.2)), 0.1, 1.0)
    beta_z = jnp.clip(jnp.exp(math.log(1.0) - 2.3025851 * jax.random.uniform(arg_keys[4], (NX, NY, NZ), jnp.float32) ** shard_levels(arg_keys[4], (NX, NY, NZ), ((0, 8), (1, 16)), -0.2, 0.2)), 0.1, 1.0)
    return dict(right_side=right_side, alpha=alpha, beta_x=beta_x, beta_y=beta_y, beta_z=beta_z)


CHEB_HIGH = 2.0
CHEB_LOW = 0.25


def apply_terms(field, below_x, above_x, below_y, above_y, below_z, above_z, alpha, beta_x, upper_x, beta_y, upper_y, beta_z, upper_z, face_scale):
    flux = beta_x * (field - below_x) + upper_x * (field - above_x)
    flux = flux + beta_y * (field - below_y) + upper_y * (field - above_y)
    flux = flux + beta_z * (field - below_z) + upper_z * (field - above_z)
    return alpha * field + face_scale * flux


def diag_terms(alpha, beta_x, upper_x, beta_y, upper_y, beta_z, upper_z, face_scale):
    return alpha + face_scale * (beta_x + upper_x + beta_y + upper_y + beta_z + upper_z)


def chebyshev(source, inverse, operate, with_residual):
    middle = 0.5 * (CHEB_HIGH + CHEB_LOW)
    spread = 0.5 * (CHEB_HIGH - CHEB_LOW)
    ratio = middle / spread
    weight_old = 1.0 / ratio
    update = inverse * source / middle
    iterate = update
    for sweep in range(1, DEGREE):
        misfit = source - operate(iterate)
        weight_new = 1.0 / (2.0 * ratio - weight_old)
        update = weight_new * weight_old * update + (2.0 * weight_new / spread) * inverse * misfit
        iterate = iterate + update
        weight_old = weight_new
    if with_residual:
        return iterate, source - operate(iterate)
    return iterate, None


def smooth_level(source, coeffs, face_scale, with_residual):
    alpha, beta_x, beta_y, beta_z = coeffs
    upper_x = jnp.roll(beta_x, -1, axis=0)
    upper_y = jnp.roll(beta_y, -1, axis=1)
    upper_z = jnp.roll(beta_z, -1, axis=2)
    inverse = 1.0 / diag_terms(alpha, beta_x, upper_x, beta_y, upper_y, beta_z, upper_z, face_scale)

    def operate(field):
        return apply_terms(field, jnp.roll(field, 1, axis=0), jnp.roll(field, -1, axis=0), jnp.roll(field, 1, axis=1), jnp.roll(field, -1, axis=1), jnp.roll(field, 1, axis=2), jnp.roll(field, -1, axis=2), alpha, beta_x, upper_x, beta_y, upper_y, beta_z, upper_z, face_scale)

    return chebyshev(source, inverse, operate, with_residual)


def restrict_cells(values):
    size_x, size_y, size_z = values.shape
    return values.reshape(size_x // 2, 2, size_y // 2, 2, size_z // 2, 2).mean(axis=(1, 3, 5))


def restrict_coeffs(coeffs):
    alpha, beta_x, beta_y, beta_z = coeffs
    size_x, size_y, size_z = alpha.shape
    shape = (size_x // 2, 2, size_y // 2, 2, size_z // 2, 2)
    coarse_x = beta_x.reshape(shape)[:, 0].mean(axis=(2, 4))
    coarse_y = beta_y.reshape(shape)[:, :, :, 0].mean(axis=(1, 4))
    coarse_z = beta_z.reshape(shape)[..., 0].mean(axis=(1, 3))
    return (restrict_cells(alpha), coarse_x, coarse_y, coarse_z)


def reference(right_side, alpha, beta_x, beta_y, beta_z):
    coeffs = (alpha, beta_x, beta_y, beta_z)
    source = right_side
    results = []
    for level in range(3):
        smoothed, misfit = smooth_level(source, coeffs, 0.25 ** level, True)
        results.append(smoothed)
        source = restrict_cells(misfit)
        coeffs = restrict_coeffs(coeffs)
    coarsest, unused = smooth_level(source, coeffs, 0.25 ** 3, False)
    return (results[0], results[1], results[2], coarsest)
```

```python
import functools

import jax
import jax.numpy as jnp
from jax import lax
from jax.experimental import pallas as pl
from jax.experimental.pallas import tpu as pltpu
from jax.sharding import PartitionSpec as P

DEGREE = 4
CHEB_HIGH = 2.0
CHEB_LOW = 0.25
LANES = 128
PAD = 8
REACH = 4
GROUP = 4
MESH = pl.DeviceIdType.MESH
F32 = jnp.float32
BF16 = jnp.bfloat16


def chebyshev_weights():
    theta = 0.5 * (CHEB_HIGH + CHEB_LOW)
    delta = 0.5 * (CHEB_HIGH - CHEB_LOW)
    sigma = theta / delta
    old = 1.0 / sigma
    first, second = [], []
    for _ in range(1, DEGREE):
        new = 1.0 / (2.0 * sigma - old)
        first.append(new * old)
        second.append(2.0 * new / delta)
        old = new
    s1 = 1.0 / theta
    s2 = second[0] * s1
    s3 = second[1] * s2
    s4 = second[2] * s3
    keep = [1.0 + first[k] - second[k] for k in range(3)]
    return (
        (((keep[0] * s1 + second[0]) / s2,), 1.0),
        ((keep[1] * s2 / s3, (second[1] - first[1] * s1) / s3), 1.0),
        ((keep[2] * s3, -first[2] * s2, second[2]), s4),
    )


WEIGHTS = chebyshev_weights()


def lane_index(shape):
    return lax.broadcasted_iota(jnp.int32, shape, len(shape) - 1)


def z_below(v):
    turned = pltpu.roll(v, 1, 2)
    if v.shape[0] == 1:
        return turned
    before = jnp.concatenate([turned[-1:], turned[:-1]], axis=0)
    return jnp.where(lane_index(v.shape) == 0, before, turned)


def z_above(v):
    turned = pltpu.roll(v, LANES - 1, 2)
    if v.shape[0] == 1:
        return turned
    after = jnp.concatenate([turned[1:], turned[:1]], axis=0)
    return jnp.where(lane_index(v.shape) == LANES - 1, after, turned)


def neighbour_sum(u, du, dr, bx, by, bz, p, r, size):
    here = pl.ds(r + dr, size)
    q = p + du
    v = u[q, :, here, :]
    depth = bz(p, r)
    total = bx(p, r) * u[q - 1, :, here, :] + bx(p + 1, r) * u[q + 1, :, here, :]
    total = total + by(p, r) * u[q, :, pl.ds(r + dr - 1, size), :]
    total = total + by(p, r + 1) * u[q, :, pl.ds(r + dr + 1, size), :]
    total = total + (depth * z_below(v) + z_above(depth * v))
    return v, total


def inverse_of(diag):
    guess = pl.reciprocal(diag, approx=True)
    return guess * (2.0 - diag * guess)


def fold(values, table):
    high = values.astype(BF16)
    low = (values - high.astype(F32)).astype(BF16)
    both = jnp.dot(jnp.concatenate([high, low], axis=0), table, preferred_element_type=F32)
    return both[: values.shape[0]] + both[values.shape[0] :]


def fold_planes(blocks, table):
    tiles, rows, _ = blocks[0].shape
    if tiles == 1:
        stacked = jnp.concatenate([block[0] for block in blocks], axis=0)
        out = fold(stacked, table)
        return [out[i * rows : (i + 1) * rows][None] for i in range(len(blocks))]
    parts = []
    for block in blocks:
        for t in range(0, tiles, 2):
            parts.append(jnp.concatenate([block[t], block[t + 1]], axis=1))
    out = fold(jnp.concatenate(parts, axis=0), table)
    half = tiles // 2
    result = []
    for i in range(len(blocks)):
        rows_of = [out[(i * half + t) * rows : (i * half + t + 1) * rows] for t in range(half)]
        result.append(jnp.stack(rows_of, axis=0))
    return result


def kernel(dims, counts, *refs):
    nx, ny, nz = dims
    tiles = nz // LANES
    refs = list(refs)
    rhs_h, alpha_h, bx_h, by_h, bz_h = refs[:5]
    outs = refs[5:9]
    f0, al0, bx0, by0, bz0, inv0, diag0, u1, u2, u3, u4, rt = refs[9:21]
    table_pair, table_even, small_pair, small_even, top = refs[21:26]
    coarse = [refs[26 + 11 * level : 26 + 11 * (level + 1)] for level in range(3)]
    in_sem, send_sem, recv_sem, out_sem = refs[59:63]

    gx, gy = lax.axis_index("gx"), lax.axis_index("gy")
    cx, cy = counts

    def device(ox, oy):
        return (lax.rem(gx + ox + cx, cx), lax.rem(gy + oy + cy, cy))

    around = [(ox, oy) for ox in (-1, 0, 1) for oy in (-1, 0, 1) if (ox, oy) != (0, 0)]

    used = [0]
    sent = []

    def send(src, dst, where):
        index = used[0]
        used[0] += 1
        copy = pltpu.make_async_remote_copy(
            src_ref=src,
            dst_ref=dst,
            send_sem=send_sem.at[index],
            recv_sem=recv_sem.at[index],
            device_id=device(*where),
            device_id_type=MESH,
        )
        copy.start()
        sent.append(copy)
        return copy

    locals_of = ((bx_h, bx0), (by_h, by0), (bz_h, bz0), (alpha_h, al0), (rhs_h, f0))
    groups = nx // GROUP
    for g in range(groups):
        for a, (src, dst) in enumerate(locals_of):
            for t in range(tiles):
                pltpu.make_async_copy(
                    src.at[pl.ds(g * GROUP, GROUP), :, pl.ds(t * LANES, LANES)],
                    dst.at[pl.ds(g * GROUP, GROUP), t, pl.ds(0, ny)],
                    in_sem.at[a, g],
                ).start()
        if g == 0:
            barrier = pltpu.get_barrier_semaphore()
            for where in around:
                pl.semaphore_signal(barrier, inc=1, device_id=device(*where), device_id_type=MESH)

    def wait_input(g):
        for a, (_, dst) in enumerate(locals_of):
            part = dst.at[pl.ds(g * GROUP, GROUP), :, pl.ds(0, ny)]
            pltpu.make_async_copy(part, part, in_sem.at[a, g]).wait()

    def fill(ref, even):
        k = lax.broadcasted_iota(jnp.int32, ref.shape, 0)
        c = lax.broadcasted_iota(jnp.int32, ref.shape, 1)
        if ref.shape[0] == LANES:
            c = c % (LANES // 2)
        hit = k == 2 * c if even else k // 2 == c
        ref[...] = jnp.where(hit, 1.0, 0.0).astype(BF16)

    fill(table_pair, False)
    fill(table_even, True)
    fill(small_pair, False)
    fill(small_even, True)

    pl.semaphore_wait(barrier, len(around))

    halo = []
    for t in range(tiles):
        lanes = pl.ds(t * LANES, LANES)
        halo.append(send(by_h.at[:, pl.ds(0, 1), lanes], by0.at[:, t, pl.ds(ny, 1)], (0, -1)))
    for t in range(tiles):
        lanes = pl.ds(t * LANES, LANES)
        halo.append(send(bx_h.at[0, :, lanes], bx0.at[nx, t], (-1, 0)))

    def start_rows(p, r, size):
        rows = pl.ds(r, size)
        depth = bz0[p, :, rows, :]
        diag = al0[p, :, rows, :] + bx0[p, :, rows, :] + bx0[p + 1, :, rows, :]
        diag = diag + by0[p, :, rows, :] + by0[p, :, pl.ds(r + 1, size), :]
        diag = diag + depth + z_above(depth)
        inverse = inverse_of(diag)
        diag0[p, :, rows, :] = diag
        inv0[p, :, rows, :] = inverse
        u1[p + 1, :, pl.ds(r + PAD, size), :] = inverse * f0[p, :, rows, :]

    def start_plane(p, _):
        for r in range(0, ny, 16):
            start_rows(p, r, 16)
        return 0

    for t in range(tiles):
        halo[t].wait_recv()
    for g in range(groups):
        wait_input(g)
        first = max(g * GROUP - 1, 0)
        last = (g + 1) * GROUP - 1
        if g == groups - 1:
            for t in range(tiles):
                halo[tiles + t].wait_recv()
            last = nx
        lax.fori_loop(first, last, start_plane, 0)

    def send_fine(u):
        rows = pl.ds(PAD, ny)
        planes = pl.ds(1, nx)
        return [
            send(u.at[1, :, rows], u.at[nx + 1, :, rows], (-1, 0)),
            send(u.at[nx, :, rows], u.at[0, :, rows], (1, 0)),
            send(u.at[planes, :, pl.ds(PAD, 1)], u.at[planes, :, pl.ds(PAD + ny, 1)], (0, -1)),
            send(u.at[planes, :, pl.ds(PAD + ny - 1, 1)], u.at[planes, :, pl.ds(PAD - 1, 1)], (0, 1)),
        ]

    flying = send_fine(u1)

    def level_dims(level):
        return nx >> level, ny >> level, max(tiles >> level, 1)

    def reach_of(level):
        return min(REACH, nx >> level)

    def pair_rows(ref, p, size):
        return ref[p, :, pl.ds(0, size, 2), :] + ref[p, :, pl.ds(1, size, 2), :]

    def restrict_block(level, source, table_p, table_e, plane_list, with_x):
        al, bx, by, bz = source
        al_c, bx_c, by_c, bz_c = coarse[level - 1][:4]
        rows = ny >> level
        more = rows + PAD
        planes = plane_list
        folded = fold_planes([pair_rows(bx, 2 * p, rows) for p in planes], table_p)
        for p, value in zip(planes, folded):
            bx_c[p, :, pl.ds(0, rows), :] = value * 0.0625
        if not with_x:
            return
        folded = fold_planes(
            [by[2 * p, :, pl.ds(0, more, 2), :] + by[2 * p + 1, :, pl.ds(0, more, 2), :] for p in planes], table_p
        )
        for p, value in zip(planes, folded):
            by_c[p, :, pl.ds(0, more), :] = value * 0.0625
        folded = fold_planes([pair_rows(bz, 2 * p, rows) + pair_rows(bz, 2 * p + 1, rows) for p in planes], table_e)
        for p, value in zip(planes, folded):
            bz_c[p, :, pl.ds(0, rows), :] = value * 0.0625
        folded = fold_planes([pair_rows(al, 2 * p, rows) + pair_rows(al, 2 * p + 1, rows) for p in planes], table_p)
        for p, value in zip(planes, folded):
            al_c[p, :, pl.ds(0, rows), :] = value * 0.125

    def coarse_plane(level, p):
        al, bx, by, bz, diag_c, ext = coarse[level - 1][:6]
        _, rows, count = level_dims(level)
        reach = reach_of(level)
        own = pl.ds(0, rows)
        lower_x, lower_y, depth = bx[p, :, own, :], by[p, :, own, :], bz[p, :, own, :]
        diag = al[p, :, own, :] + lower_x + bx[p + 1, :, own, :]
        diag = diag + lower_y + by[p, :, pl.ds(1, rows), :] + depth + z_above(depth)
        diag_c[p, :, :, :] = diag
        place = pl.ds(PAD, rows)
        for a, value in enumerate((lower_x, lower_y, depth, inverse_of(diag))):
            ext[p + reach, pl.ds(a * count, count), place, :] = value

    def send_wide_x(level):
        ext = coarse[level - 1][5]
        planes, rows, _ = level_dims(level)
        reach = reach_of(level)
        own = pl.ds(PAD, rows)
        return [
            send(ext.at[pl.ds(reach, reach), :, own], ext.at[pl.ds(reach + planes, reach), :, own], (-1, 0)),
            send(ext.at[pl.ds(planes, reach), :, own], ext.at[pl.ds(0, reach), :, own], (1, 0)),
        ]

    def send_wide_y(level):
        ext = coarse[level - 1][5]
        _, rows, _ = level_dims(level)
        return [
            send(ext.at[:, :, pl.ds(PAD, REACH)], ext.at[:, :, pl.ds(PAD + rows, REACH)], (0, -1)),
            send(ext.at[:, :, pl.ds(PAD + rows - REACH, REACH)], ext.at[:, :, pl.ds(PAD - REACH, REACH)], (0, 1)),
        ]

    wide = {}
    fine_coeffs = (al0, bx0, by0, bz0)

    def first_coarse(p, _):
        restrict_block(1, fine_coeffs, table_pair[...], table_even[...], [p], True)
        return 0

    lax.fori_loop(0, nx // 2, first_coarse, 0)
    restrict_block(1, fine_coeffs, table_pair[...], table_even[...], [nx // 2], False)

    def first_plane(p, _):
        coarse_plane(1, p)
        return 0

    lax.fori_loop(0, nx // 2, first_plane, 0)
    wide[1] = send_wide_x(1)
    for level in (2, 3):
        tables = (table_pair, table_even) if level == 2 else (small_pair, small_even)
        planes = nx >> level
        source = coarse[level - 2][:4]
        restrict_block(level, source, tables[0][...], tables[1][...], list(range(planes)), True)
        restrict_block(level, source, tables[0][...], tables[1][...], [planes], False)
        for p in range(planes):
            coarse_plane(level, p)
        wide[level] = send_wide_x(level)

    def fine_face(ref, size):
        return lambda p, r: ref[p, :, pl.ds(r, size), :]

    def fine_sum(u, p, r, size):
        return neighbour_sum(u, 1, PAD, fine_face(bx0, size), fine_face(by0, size), fine_face(bz0, size), p, r, size)

    def combine(weights, v, total, inverse, older):
        factors, scale = weights
        change = inverse * total
        if scale != 1.0:
            change = change * scale
        value = factors[0] * v
        for factor, field in zip(factors[1:], older):
            value = value + factor * field
        return value + change

    def fine_sweep(weights, fields, target):
        u, older = fields[0], fields[1:]

        def update(p, r, size):
            v, total = fine_sum(u, p, r, size)
            place = pl.ds(r + PAD, size)
            past = [field[p + 1, :, place, :] for field in older]
            target[p + 1, :, place, :] = combine(weights, v, total, inv0[p, :, pl.ds(r, size), :], past)

        def end_planes(j, _):
            r = pl.multiple_of(j * 8, 8)
            update(0, r, 8)
            update(nx - 1, r, 8)
            return 0

        def end_rows(p, _):
            update(p, 0, 8)
            update(p, ny - 8, 8)
            return 0

        def inner(p, _):
            for r in range(8, ny - 8, 16):
                update(p, r, 16)
            return 0

        lax.fori_loop(0, ny // 8, end_planes, 0)
        lax.fori_loop(1, nx - 1, end_rows, 0)
        copies = send_fine(target)
        lax.fori_loop(1, nx - 1, inner, 0)
        return copies

    fields = [u1]
    for k, target in enumerate((u2, u3, u4)):
        for copy in flying:
            copy.wait_recv()
        flying = fine_sweep(WEIGHTS[k], fields, target)
        fields.insert(0, target)
        if k == 0:
            for level in (1, 2, 3):
                for copy in wide[level]:
                    copy.wait_recv()
            wide = {level: send_wide_y(level) for level in (1, 2, 3)}

    stores = []

    def store(src, dst, index):
        copy = pltpu.make_async_copy(src, dst, out_sem.at[index])
        copy.start()
        stores.append(copy)

    for t in range(tiles):
        store(u4.at[pl.ds(1, nx), t, pl.ds(PAD, ny)], outs[0].at[:, :, pl.ds(t * LANES, LANES)], t)

    for copy in flying:
        copy.wait_recv()

    def fine_residual(p, r, size):
        v, total = fine_sum(u4, p, r, size)
        rows = pl.ds(r, size)
        return f0[p, :, rows, :] - diag0[p, :, rows, :] * v + total

    def residual_pair(p, _):
        for r in range(0, ny, 8):
            rt[p, :, pl.ds(r, 8), :] = fine_residual(2 * p, r, 8) + fine_residual(2 * p + 1, r, 8)
        return 0

    def send_source(level, ox):
        field = coarse[level - 1][6]
        planes, rows, _ = level_dims(level)
        reach = reach_of(level)
        from_x = {-1: reach, 0: reach, 1: planes}[ox]
        to_x = {-1: reach + planes, 0: reach, 1: 0}[ox]
        depth = planes if ox == 0 else reach
        copies = []
        for oy in (0, -1, 1):
            if (ox, oy) == (0, 0):
                continue
            from_y = {-1: PAD, 0: PAD, 1: PAD + rows - REACH}[oy]
            to_y = {-1: PAD + rows, 0: PAD, 1: PAD - REACH}[oy]
            width = rows if oy == 0 else REACH
            copies.append(
                send(
                    field.at[pl.ds(from_x, depth), :, pl.ds(from_y, width)],
                    field.at[pl.ds(to_x, depth), :, pl.ds(to_y, width)],
                    (ox, oy),
                )
            )
        return copies

    def first_source(p, _):
        value = fold_planes([pair_rows(rt, p, ny // 2)], table_pair[...])[0]
        coarse[0][6][p + reach_of(1), :, pl.ds(PAD, ny // 2), :] = value * 0.125
        return 0

    flying = []
    half = nx // 2
    for low, high, ox in ((0, REACH, -1), (half - REACH, half, 1), (REACH, half - REACH, 0)):
        lax.fori_loop(low, high, residual_pair, 0)
        lax.fori_loop(low, high, first_source, 0)
        flying += send_source(1, ox)

    for level in (1, 2, 3):
        for copy in wide[level]:
            copy.wait_recv()

    def solve(level):
        diag_c, ext, src, c1, c2, c3, c4 = coarse[level - 1][4:11]
        planes, rows, count = level_dims(level)
        reach = reach_of(level)
        whole = planes + 2 * reach
        window = pl.ds(PAD - REACH, rows + 2 * REACH)
        size = rows + 2 * REACH
        unroll = 1 if level == 1 else True

        def face(a, size):
            return lambda p, r: ext[p, pl.ds(a * count, count), pl.ds(r, size), :]

        def start(p, _):
            c1[p, :, window, :] = ext[p, pl.ds(3 * count, count), window, :] * src[p, :, window, :]
            return 0

        lax.fori_loop(0, whole, start, 0, unroll=unroll)
        chain = [c1]
        for k, target in enumerate((c2, c3, c4)):
            u, older = chain[0], chain[1:]
            if k == 2 and level == 3:
                first, place, length = PAD, pl.ds(PAD, rows), rows
            else:
                first, place, length = PAD - REACH, window, size

            def sweep(p, _):
                v, total = neighbour_sum(u, 0, 0, face(0, length), face(1, length), face(2, length), p, first, length)
                past = [field[p, :, place, :] for field in older]
                inverse = ext[p, pl.ds(3 * count, count), place, :]
                target[p, :, place, :] = combine(WEIGHTS[k], v, total, inverse, past)
                return 0

            lax.fori_loop(k + 1, whole - k - 1, sweep, 0, unroll=unroll)
            chain.insert(0, target)

        if level == 3:
            return

        def residual(p):
            v, total = neighbour_sum(
                c4, 0, 0, face(0, rows), face(1, rows), face(2, rows), p + reach, PAD, rows
            )
            return src[p + reach, :, pl.ds(PAD, rows), :] - diag_c[p] * v + total

        def pair(p, _):
            c2[p, :, pl.ds(0, rows), :] = residual(2 * p) + residual(2 * p + 1)
            return 0

        lax.fori_loop(0, planes // 2, pair, 0, unroll=unroll)
        table = table_pair if level == 1 else small_pair
        folded = fold_planes([pair_rows(c2, p, rows // 2) for p in range(planes // 2)], table[...])
        for p, value in enumerate(folded):
            coarse[level][6][p + reach_of(level + 1), :, pl.ds(PAD, rows // 2), :] = value * 0.125

    for level in (1, 2, 3):
        for copy in flying:
            copy.wait_recv()
        solve(level)
        planes, rows, count = level_dims(level)
        own_planes = pl.ds(reach_of(level), planes)
        result = coarse[level - 1][10]
        if level < 3:
            flying = send_source(level + 1, -1) + send_source(level + 1, 1) + send_source(level + 1, 0)
            for t in range(count):
                store(
                    result.at[own_planes, t, pl.ds(PAD, rows)],
                    outs[level].at[:, :, pl.ds(t * LANES, LANES)],
                    tiles * level + t,
                )
        else:
            top[...] = result[own_planes, 0, pl.ds(PAD, rows), pl.ds(0, LANES // 2)]
            store(top, outs[3], 3 * tiles)

    for copy in sent:
        copy.wait_send()
    for copy in stores:
        copy.wait()


def scratch_of(dims):
    nx, ny, nz = dims
    tiles = nz // LANES

    def space(*shape):
        return pltpu.VMEM(shape, F32)

    shapes = [
        space(nx, tiles, ny, LANES),
        space(nx, tiles, ny, LANES),
        space(nx + 1, tiles, ny, LANES),
        space(nx, tiles, ny + 2 * PAD, LANES),
        space(nx, tiles, ny, LANES),
        space(nx, tiles, ny, LANES),
        space(nx, tiles, ny, LANES),
    ]
    shapes += [space(nx + 2, tiles, ny + 2 * PAD, LANES)] * 4
    shapes += [space(nx // 2, tiles, ny, LANES)]
    shapes += [pltpu.VMEM((2 * LANES, LANES), BF16)] * 2
    shapes += [pltpu.VMEM((LANES, LANES), BF16)] * 2
    shapes += [space(nx // 8, ny // 8, LANES // 2)]
    for level in (1, 2, 3):
        x, y, t = nx >> level, ny >> level, max(tiles >> level, 1)
        whole = x + 2 * min(REACH, x)
        tall = y + 2 * PAD
        shapes += [
            space(x, t, y, LANES),
            space(x + 1, t, y, LANES),
            space(x, t, tall, LANES),
            space(x, t, y, LANES),
            space(x, t, y, LANES),
            space(whole, 4 * t, tall, LANES),
        ]
        shapes += [space(whole, t, tall, LANES)] * 5
    shapes += [
        pltpu.SemaphoreType.DMA((5, nx // GROUP)),
        pltpu.SemaphoreType.DMA((64,)),
        pltpu.SemaphoreType.DMA((64,)),
        pltpu.SemaphoreType.DMA((16,)),
    ]
    return shapes


def body(counts, *args):
    dims = args[0].shape
    nx, ny, nz = dims
    return pl.pallas_call(
        functools.partial(kernel, dims, counts),
        out_shape=[jax.ShapeDtypeStruct((nx >> k, ny >> k, nz >> k), F32) for k in range(4)],
        in_specs=[pl.BlockSpec(memory_space=pl.ANY)] * 5,
        out_specs=[pl.BlockSpec(memory_space=pl.ANY)] * 4,
        scratch_shapes=scratch_of(dims),
        compiler_params=pltpu.CompilerParams(
            collective_id=0, has_side_effects=True, vmem_limit_bytes=60 * 2**20
        ),
        name="sweep",
    )(*args)


def solution(mesh):
    spec = P("gx", "gy", None)
    counts = (mesh.shape["gx"], mesh.shape["gy"])
    return jax.shard_map(
        functools.partial(body, counts),
        mesh=mesh,
        in_specs=(spec,) * 5,
        out_specs=(spec,) * 4,
        check_vma=False,
    )
```

```python
import functools

import jax
import jax.numpy as jnp
from jax import lax
from jax.experimental import pallas as pl
from jax.experimental.pallas import tpu as pltpu
from jax.sharding import PartitionSpec as P

DEGREE = 4
CHEB_HIGH = 2.0
CHEB_LOW = 0.25
LANES = 128
PAD = 8
REACH = 4
GROUPS = 4
MESH = pl.DeviceIdType.MESH
F32 = jnp.float32
BF16 = jnp.bfloat16


def chebyshev_weights():
    theta = 0.5 * (CHEB_HIGH + CHEB_LOW)
    delta = 0.5 * (CHEB_HIGH - CHEB_LOW)
    sigma = theta / delta
    old = 1.0 / sigma
    first, second = [], []
    for _ in range(1, DEGREE):
        new = 1.0 / (2.0 * sigma - old)
        first.append(new * old)
        second.append(2.0 * new / delta)
        old = new
    s1 = 1.0 / theta
    s2 = second[0] * s1
    s3 = second[1] * s2
    s4 = second[2] * s3
    keep = [1.0 + first[k] - second[k] for k in range(3)]
    return (
        (((keep[0] * s1 + second[0]) / s2,), 1.0),
        ((keep[1] * s2 / s3, (second[1] - first[1] * s1) / s3), 1.0),
        ((keep[2] * s3, -first[2] * s2, second[2]), s4),
    )


WEIGHTS = chebyshev_weights()


def loop(low, high, step, fn):
    turns = (high - low) // step

    def turn(i, _):
        for k in range(step):
            fn(low + i * step + k)
        return 0

    if turns == 1:
        turn(0, 0)
    elif turns:
        lax.fori_loop(0, turns, turn, 0)
    for k in range(low + turns * step, high):
        fn(k)


def lane_index(shape):
    return lax.broadcasted_iota(jnp.int32, shape, len(shape) - 1)


def z_below(v):
    turned = pltpu.roll(v, 1, 2)
    if v.shape[0] == 1:
        return turned
    before = jnp.concatenate([turned[-1:], turned[:-1]], axis=0)
    return jnp.where(lane_index(v.shape) == 0, before, turned)


def z_above(v):
    turned = pltpu.roll(v, LANES - 1, 2)
    if v.shape[0] == 1:
        return turned
    after = jnp.concatenate([turned[1:], turned[:1]], axis=0)
    return jnp.where(lane_index(v.shape) == LANES - 1, after, turned)


def neighbour_sum(u, du, dr, bx, by, bz, p, r, size):
    here = pl.ds(r + dr, size)
    q = p + du
    v = u[q, :, here, :]
    depth = bz(p, r)
    total = bx(p, r) * u[q - 1, :, here, :] + bx(p + 1, r) * u[q + 1, :, here, :]
    total = total + by(p, r) * u[q, :, pl.ds(r + dr - 1, size), :]
    total = total + by(p, r + 1) * u[q, :, pl.ds(r + dr + 1, size), :]
    total = total + (depth * z_below(v) + z_above(depth * v))
    return v, total


def inverse_of(diag):
    guess = pl.reciprocal(diag, approx=True)
    return guess * (2.0 - diag * guess)


def fold(values, table):
    high = values.astype(BF16)
    low = (values - high.astype(F32)).astype(BF16)
    both = jnp.dot(jnp.concatenate([high, low], axis=0), table, preferred_element_type=F32)
    return both[: values.shape[0]] + both[values.shape[0] :]


def fold_planes(blocks, table):
    tiles, rows, _ = blocks[0].shape
    if tiles == 1:
        stacked = jnp.concatenate([block[0] for block in blocks], axis=0)
        out = fold(stacked, table)
        return [out[i * rows : (i + 1) * rows][None] for i in range(len(blocks))]
    parts = []
    for block in blocks:
        for t in range(0, tiles, 2):
            parts.append(jnp.concatenate([block[t], block[t + 1]], axis=1))
    out = fold(jnp.concatenate(parts, axis=0), table)
    half = tiles // 2
    result = []
    for i in range(len(blocks)):
        rows_of = [out[(i * half + t) * rows : (i * half + t + 1) * rows] for t in range(half)]
        result.append(jnp.stack(rows_of, axis=0))
    return result


def level_dims(dims, level):
    nx, ny, nz = dims
    return nx >> level, ny >> level, max((nz // LANES) >> level, 1)


def reach_of(dims, level):
    return min(REACH, dims[0] >> level)


def combine(weights, v, total, inverse, older):
    factors, scale = weights
    change = inverse * total
    if scale != 1.0:
        change = change * scale
    value = factors[0] * v
    for factor, field in zip(factors[1:], older):
        value = value + factor * field
    return value + change


def wide_sweeps(dims, level, ext, chain, targets):
    planes, rows, count = level_dims(dims, level)
    whole = planes + 2 * reach_of(dims, level)
    step = 6 if level == 1 else whole
    chain = list(chain)
    for k, target in enumerate(targets):
        u, older = chain[0], chain[1:]
        if k == 2 and level == 3:
            first, length = PAD, rows
        else:
            first, length = PAD - REACH, rows + 2 * REACH
        place = pl.ds(first, length)

        def sweep(p):
            v, total = neighbour_sum(u, 0, 0, *coarse_faces(ext, count, length), p, first, length)
            past = [field[p, :, place, :] for field in older]
            inverse = ext[p, pl.ds(3 * count, count), place, :]
            target[p, :, place, :] = combine(WEIGHTS[k], v, total, inverse, past)

        loop(k + 1, whole - k - 1, step, sweep)
        chain.insert(0, target)


def coarse_faces(ext, count, length):
    def face(a):
        return lambda p, r: ext[p, pl.ds(a * count, count), pl.ds(r, length), :]

    return face(0), face(1), face(2)


def kernel(dims, counts, *refs):
    nx, ny, nz = dims
    tiles = nz // LANES
    refs = list(refs)
    rhs_h, alpha_h, bx_h, by_h, bz_h = refs[:5]
    u4, mid, low, ext3, first3 = refs[5:10]
    f0, al0, bx0, by0, bz0, inv0, diag0, u1, u2, u3 = refs[10:20]
    rt = al0
    table_pair, table_even, small_pair, small_even = refs[20:24]
    coarse = [refs[24:34] + [mid], refs[34:44] + [low], refs[44:49] + [ext3, None, first3]]
    in_sem, send_sem, recv_sem = refs[49:52]

    gx, gy = lax.axis_index("gx"), lax.axis_index("gy")
    cx, cy = counts

    def device(ox, oy):
        return (lax.rem(gx + ox + cx, cx), lax.rem(gy + oy + cy, cy))

    around = [(ox, oy) for ox in (-1, 0, 1) for oy in (-1, 0, 1) if (ox, oy) != (0, 0)]

    used = [0]
    sent = []

    def send(src, dst, where):
        index = used[0]
        used[0] += 1
        copy = pltpu.make_async_remote_copy(
            src_ref=src,
            dst_ref=dst,
            send_sem=send_sem.at[index],
            recv_sem=recv_sem.at[index],
            device_id=device(*where),
            device_id_type=MESH,
        )
        copy.start()
        sent.append(copy)
        return copy

    locals_of = ((bx_h, bx0), (by_h, by0), (bz_h, bz0), (alpha_h, al0), (rhs_h, f0))
    edge = 8
    inner_rows = (edge, ny - edge)
    cuts = [1 + (nx - 2) * g // GROUPS for g in range(GROUPS + 1)]

    def pieces(a):
        low = 2 * edge if a == 1 else edge
        ahead = 2 if a == 0 else 1
        parts = [((0, nx), (0, low)), ((0, nx), (ny - edge, ny))]
        parts += [((0, ahead), (low, ny - edge)), ((nx - 1, nx), (low, ny - edge))]
        for g in range(GROUPS):
            start = max(cuts[g], ahead)
            parts.append(((start, cuts[g + 1]), (low, ny - edge)))
        return parts

    def part_of(ref, planes, rows):
        return ref.at[pl.ds(planes[0], planes[1] - planes[0]), :, pl.ds(rows[0], rows[1] - rows[0])]

    def load(n):
        for a, (src, dst) in enumerate(locals_of):
            planes, rows = pieces(a)[n]
            for t in range(tiles):
                pltpu.make_async_copy(
                    part_of(src, planes, (t * LANES, (t + 1) * LANES)).at[:, pl.ds(rows[0], rows[1] - rows[0])],
                    part_of(dst, planes, rows).at[:, t],
                    in_sem.at[a, n],
                ).start()

    def wait_input(n):
        for a, (_, dst) in enumerate(locals_of):
            part = part_of(dst, *pieces(a)[n])
            pltpu.make_async_copy(part, part, in_sem.at[a, n]).wait()

    barrier = pltpu.get_barrier_semaphore()
    for where in around:
        pl.semaphore_signal(barrier, inc=1, device_id=device(*where), device_id_type=MESH)
    for n in range(4 + GROUPS):
        load(n)

    def fill(ref, even):
        k = lax.broadcasted_iota(jnp.int32, ref.shape, 0)
        c = lax.broadcasted_iota(jnp.int32, ref.shape, 1)
        if ref.shape[0] == LANES:
            c = c % (LANES // 2)
        hit = k == 2 * c if even else k // 2 == c
        ref[...] = jnp.where(hit, 1.0, 0.0).astype(BF16)

    fill(table_pair, False)
    fill(table_even, True)
    fill(small_pair, False)
    fill(small_even, True)

    pl.semaphore_wait(barrier, len(around))

    halo = []
    for t in range(tiles):
        lanes = pl.ds(t * LANES, LANES)
        halo.append(send(by_h.at[:, pl.ds(0, 1), lanes], by0.at[:, t, pl.ds(ny, 1)], (0, -1)))
    for t in range(tiles):
        lanes = pl.ds(t * LANES, LANES)
        halo.append(send(bx_h.at[0, :, lanes], bx0.at[nx, t], (-1, 0)))

    def start_rows(p, r, size):
        rows = pl.ds(r, size)
        depth = bz0[p, :, rows, :]
        diag = al0[p, :, rows, :] + bx0[p, :, rows, :] + bx0[p + 1, :, rows, :]
        diag = diag + by0[p, :, rows, :] + by0[p, :, pl.ds(r + 1, size), :]
        diag = diag + depth + z_above(depth)
        inverse = inverse_of(diag)
        diag0[p, :, rows, :] = diag
        inv0[p, :, rows, :] = inverse
        u1[p + 1, :, pl.ds(r + PAD, size), :] = inverse * f0[p, :, rows, :]

    def start_ends(j):
        r = pl.multiple_of(j * 16, 16)
        start_rows(0, r, 16)
        start_rows(nx - 1, r, 16)

    def start_edges(p):
        start_rows(p, 0, 8)
        start_rows(p, ny - 8, 8)

    def start_inner(p):
        for r in range(8, ny - 8, 16):
            start_rows(p, r, 16)

    def send_planes(u):
        rows = pl.ds(PAD, ny)
        return [
            send(u.at[1, :, rows], u.at[nx + 1, :, rows], (-1, 0)),
            send(u.at[nx, :, rows], u.at[0, :, rows], (1, 0)),
        ]

    def send_rows(u):
        planes = pl.ds(1, nx)
        return [
            send(u.at[planes, :, pl.ds(PAD, 1)], u.at[planes, :, pl.ds(PAD + ny, 1)], (0, -1)),
            send(u.at[planes, :, pl.ds(PAD + ny - 1, 1)], u.at[planes, :, pl.ds(PAD - 1, 1)], (0, 1)),
        ]

    def land(copies):
        for copy in copies:
            copy.wait_recv()

    for n in range(4):
        wait_input(n)
    land(halo)
    loop(0, ny // 16, 2, start_ends)
    flying = send_planes(u1)
    loop(1, nx - 1, 4, start_edges)
    flying += send_rows(u1)
    for g in range(GROUPS):
        wait_input(4 + g)
        last = nx - 1 if g == GROUPS - 1 else cuts[g + 1] - 1
        loop(max(cuts[g] - 1, 1), last, 2, start_inner)

    def pair_rows(ref, p, size):
        return ref[p, :, pl.ds(0, size, 2), :] + ref[p, :, pl.ds(1, size, 2), :]

    def restrict_block(level, source, table_p, table_e, plane_list, with_x):
        al, bx, by, bz = source
        al_c, bx_c, by_c, bz_c = coarse[level - 1][:4]
        rows = ny >> level
        more = rows + PAD
        planes = plane_list
        folded = fold_planes([pair_rows(bx, 2 * p, rows) for p in planes], table_p)
        for p, value in zip(planes, folded):
            bx_c[p, :, pl.ds(0, rows), :] = value * 0.0625
        if not with_x:
            return
        folded = fold_planes(
            [by[2 * p, :, pl.ds(0, more, 2), :] + by[2 * p + 1, :, pl.ds(0, more, 2), :] for p in planes], table_p
        )
        for p, value in zip(planes, folded):
            by_c[p, :, pl.ds(0, more), :] = value * 0.0625
        folded = fold_planes([pair_rows(bz, 2 * p, rows) + pair_rows(bz, 2 * p + 1, rows) for p in planes], table_e)
        for p, value in zip(planes, folded):
            bz_c[p, :, pl.ds(0, rows), :] = value * 0.0625
        folded = fold_planes([pair_rows(al, 2 * p, rows) + pair_rows(al, 2 * p + 1, rows) for p in planes], table_p)
        for p, value in zip(planes, folded):
            al_c[p, :, pl.ds(0, rows), :] = value * 0.125

    def coarse_plane(level, p):
        al, bx, by, bz, diag_c, ext = coarse[level - 1][:6]
        _, rows, count = level_dims(dims, level)
        reach = reach_of(dims, level)
        own = pl.ds(0, rows)
        lower_x, lower_y, depth = bx[p, :, own, :], by[p, :, own, :], bz[p, :, own, :]
        diag = al[p, :, own, :] + lower_x + bx[p + 1, :, own, :]
        diag = diag + lower_y + by[p, :, pl.ds(1, rows), :] + depth + z_above(depth)
        diag_c[p, :, :, :] = diag
        place = pl.ds(PAD, rows)
        for a, value in enumerate((lower_x, lower_y, depth, inverse_of(diag))):
            ext[p + reach, pl.ds(a * count, count), place, :] = value

    def send_wide_x(level, arrays):
        ext = coarse[level - 1][5]
        planes, rows, count = level_dims(dims, level)
        reach = reach_of(dims, level)
        own = pl.ds(PAD, rows)
        part = pl.ds(arrays[0] * count, (arrays[1] - arrays[0]) * count)
        return [
            send(ext.at[pl.ds(reach, reach), part, own], ext.at[pl.ds(reach + planes, reach), part, own], (-1, 0)),
            send(ext.at[pl.ds(planes, reach), part, own], ext.at[pl.ds(0, reach), part, own], (1, 0)),
        ]

    def send_wide_y(level):
        ext = coarse[level - 1][5]
        _, rows, _ = level_dims(dims, level)
        return [
            send(ext.at[:, :, pl.ds(PAD, REACH)], ext.at[:, :, pl.ds(PAD + rows, REACH)], (0, -1)),
            send(ext.at[:, :, pl.ds(PAD + rows - REACH, REACH)], ext.at[:, :, pl.ds(PAD - REACH, REACH)], (0, 1)),
        ]

    fine_coeffs = (al0, bx0, by0, bz0)

    def first_coarse(p):
        restrict_block(1, fine_coeffs, table_pair[...], table_even[...], [2 * p, 2 * p + 1], True)

    loop(0, nx // 4, 1, first_coarse)
    restrict_block(1, fine_coeffs, table_pair[...], table_even[...], [nx // 2], False)

    def first_plane(p):
        coarse_plane(1, p)

    loop(0, nx // 2, 4, first_plane)

    def lower_coarse():
        for level in (2, 3):
            tables = (table_pair, table_even) if level == 2 else (small_pair, small_even)
            planes = nx >> level
            source = coarse[level - 2][:4]
            restrict_block(level, source, tables[0][...], tables[1][...], list(range(planes)), True)
            restrict_block(level, source, tables[0][...], tables[1][...], [planes], False)
            for p in range(planes):
                coarse_plane(level, p)

    def fine_face(ref, size):
        return lambda p, r: ref[p, :, pl.ds(r, size), :]

    def fine_sum(u, p, r, size):
        return neighbour_sum(u, 1, PAD, fine_face(bx0, size), fine_face(by0, size), fine_face(bz0, size), p, r, size)

    def fine_sweep(weights, fields, target):
        u, older = fields[0], fields[1:]

        def update(p, r, size):
            v, total = fine_sum(u, p, r, size)
            place = pl.ds(r + PAD, size)
            past = [field[p + 1, :, place, :] for field in older]
            target[p + 1, :, place, :] = combine(weights, v, total, inv0[p, :, pl.ds(r, size), :], past)

        def end_planes(j):
            r = pl.multiple_of(j * 16, 16)
            update(0, r, 16)
            update(nx - 1, r, 16)

        def end_rows(p):
            update(p, 0, 8)
            update(p, ny - 8, 8)

        def inner(p):
            for r in range(8, ny - 8, 16):
                update(p, r, 16)

        loop(0, ny // 16, 2, end_planes)
        copies = send_planes(target)
        loop(1, nx - 1, 4, end_rows)
        return copies + send_rows(target), lambda: loop(1, nx - 1, 4, inner)

    fields = [u1]
    wide = []
    for k, target in enumerate((u2, u3, u4)):
        land(flying)
        flying, rest = fine_sweep(WEIGHTS[k], fields, target)
        if k == 0:
            wide += send_wide_x(1, (0, 2))
        elif k == 1:
            wide += send_wide_x(1, (2, 4)) + send_wide_x(2, (0, 4)) + send_wide_x(3, (0, 4))
        else:
            land(wide)
            wide = send_wide_y(1) + send_wide_y(2) + send_wide_y(3)
        rest()
        if k == 0:
            lower_coarse()
        fields.insert(0, target)

    def fine_residual(p, r, size):
        v, total = fine_sum(u4, p, r, size)
        rows = pl.ds(r, size)
        return f0[p, :, rows, :] - diag0[p, :, rows, :] * v + total

    def residual_rows(p, rows):
        for r in rows:
            rt[p, :, pl.ds(r, 8), :] = fine_residual(2 * p, r, 8) + fine_residual(2 * p + 1, r, 8)

    def residual_whole(j):
        r = pl.multiple_of(j * 8, 8)
        residual_rows(0, [r])
        residual_rows(nx // 2 - 1, [r])

    def residual_edges(p):
        residual_rows(p, (0, ny - 8))

    def residual_inner(p):
        residual_rows(p, range(8, ny - 8, 8))

    loop(1, nx // 2 - 1, 2, residual_inner)
    land(flying)
    loop(0, ny // 8, 2, residual_whole)
    loop(1, nx // 2 - 1, 5, residual_edges)

    def send_source(level, ox):
        field = coarse[level - 1][7]
        planes, rows, _ = level_dims(dims, level)
        reach = reach_of(dims, level)
        from_x = {-1: reach, 0: reach, 1: planes}[ox]
        to_x = {-1: reach + planes, 0: reach, 1: 0}[ox]
        depth = planes if ox == 0 else reach
        copies = []
        for oy in (0, -1, 1):
            if (ox, oy) == (0, 0):
                continue
            from_y = {-1: PAD, 0: PAD, 1: PAD + rows - REACH}[oy]
            to_y = {-1: PAD + rows, 0: PAD, 1: PAD - REACH}[oy]
            width = rows if oy == 0 else REACH
            copies.append(
                send(
                    field.at[pl.ds(from_x, depth), :, pl.ds(from_y, width)],
                    field.at[pl.ds(to_x, depth), :, pl.ds(to_y, width)],
                    (ox, oy),
                )
            )
        return copies

    def put_source(level, p, value):
        _, rows, count = level_dims(dims, level)
        ext, source, first = coarse[level - 1][5:8]
        q = p + reach_of(dims, level)
        own = pl.ds(PAD, rows)
        value = value * 0.125
        if source is not None:
            source[p] = value
        first[q, :, own, :] = ext[q, pl.ds(3 * count, count), own, :] * value

    def first_source(low):
        planes = range(low, low + REACH)
        folded = fold_planes([pair_rows(rt, p, ny // 2) for p in planes], table_pair[...])
        for p, value in zip(planes, folded):
            put_source(1, p, value)

    flying = []
    half = nx // 2
    for low_p, ox in ((0, -1), (half - REACH, 1)):
        first_source(low_p)
        flying += send_source(1, ox)
    for low_p in range(REACH, half - REACH, REACH):
        first_source(low_p)
    flying += send_source(1, 0)

    land(wide)
    for level in (1, 2):
        land(flying)
        diag_c, ext, source, c1, c2, c3, c4 = coarse[level - 1][4:11]
        wide_sweeps(dims, level, ext, [c1], (c2, c3, c4))
        planes, rows, count = level_dims(dims, level)
        reach = reach_of(dims, level)
        faces = coarse_faces(ext, count, rows)

        def residual(p):
            v, total = neighbour_sum(c4, 0, 0, *faces, p + reach, PAD, rows)
            return source[p] - diag_c[p] * v + total

        def pair(p):
            c2[p, :, pl.ds(0, rows), :] = residual(2 * p) + residual(2 * p + 1)

        loop(0, planes // 2, 3, pair)
        table = table_pair if level == 1 else small_pair
        folded = fold_planes([pair_rows(c2, p, rows // 2) for p in range(planes // 2)], table[...])
        for p, value in enumerate(folded):
            put_source(level + 1, p, value)
        flying = send_source(level + 1, -1) + send_source(level + 1, 1) + send_source(level + 1, 0)
    land(flying)
    for copy in sent:
        copy.wait_send()


def last_kernel(dims, u4, mid, low, ext3, first3, *refs):
    outs, (c2, c3, c4, top, sem) = refs[:4], refs[4:]
    stores = []
    for level, field in enumerate((u4, mid, low)):
        planes, rows, count = level_dims(dims, level)
        own = pl.ds(reach_of(dims, level) if level else 1, planes)
        for t in range(count):
            copy = pltpu.make_async_copy(
                field.at[own, t, pl.ds(PAD, rows)],
                outs[level].at[:, :, pl.ds(t * LANES, LANES)],
                sem.at[len(stores)],
            )
            copy.start()
            stores.append(copy)
    wide_sweeps(dims, 3, ext3, [first3], (c2, c3, c4))
    planes, rows, _ = level_dims(dims, 3)
    top[...] = c4[pl.ds(reach_of(dims, 3), planes), 0, pl.ds(PAD, rows), pl.ds(0, LANES // 2)]
    copy = pltpu.make_async_copy(top, outs[3], sem.at[len(stores)])
    copy.start()
    for store in stores + [copy]:
        store.wait()


def space(*shape):
    return pltpu.VMEM(shape, F32)


def halo_shape(dims, level):
    x, y, t = level_dims(dims, level)
    around = reach_of(dims, level) if level else 1
    return (x + 2 * around, t, y + 2 * PAD, LANES)


def scratch_of(dims):
    nx, ny, nz = dims
    tiles = nz // LANES
    shapes = [
        space(nx, tiles, ny, LANES),
        space(nx, tiles, ny, LANES),
        space(nx + 1, tiles, ny, LANES),
        space(nx, tiles, ny + 2 * PAD, LANES),
        space(nx, tiles, ny, LANES),
        space(nx, tiles, ny, LANES),
        space(nx, tiles, ny, LANES),
    ]
    shapes += [space(*halo_shape(dims, 0))] * 3
    shapes += [pltpu.VMEM((2 * LANES, LANES), BF16)] * 2
    shapes += [pltpu.VMEM((LANES, LANES), BF16)] * 2
    for level in (1, 2, 3):
        x, y, t = level_dims(dims, level)
        tall = y + 2 * PAD
        shapes += [
            space(x, t, y, LANES),
            space(x + 1, t, y, LANES),
            space(x, t, tall, LANES),
            space(x, t, y, LANES),
            space(x, t, y, LANES),
        ]
        if level < 3:
            whole = halo_shape(dims, level)
            shapes += [space(whole[0], 4 * t, tall, LANES), space(x, t, y, LANES)]
            shapes += [space(*whole)] * 3
    shapes += [
        pltpu.SemaphoreType.DMA((5, 4 + GROUPS)),
        pltpu.SemaphoreType.DMA((64,)),
        pltpu.SemaphoreType.DMA((64,)),
    ]
    return shapes


def body(counts, *args):
    dims = args[0].shape
    nx, ny, nz = dims
    whole3 = halo_shape(dims, 3)
    kept = [halo_shape(dims, level) for level in range(3)]
    kept += [(whole3[0], 4) + whole3[2:], whole3]
    in_hbm = pl.BlockSpec(memory_space=pltpu.HBM)
    in_vmem = pl.BlockSpec(memory_space=pltpu.VMEM)
    fields = pl.pallas_call(
        functools.partial(kernel, dims, counts),
        out_shape=[pltpu.VMEM(shape, F32) for shape in kept],
        in_specs=[in_hbm] * 5,
        out_specs=[in_vmem] * 5,
        scratch_shapes=scratch_of(dims),
        compiler_params=pltpu.CompilerParams(
            collective_id=0, has_side_effects=True, vmem_limit_bytes=48 * 2**20
        ),
        name="sweep",
    )(*[pltpu.with_memory_space_constraint(x, pltpu.HBM) for x in args])
    return pl.pallas_call(
        functools.partial(last_kernel, dims),
        out_shape=[pltpu.HBM((nx >> k, ny >> k, nz >> k), F32) for k in range(4)],
        in_specs=[in_vmem] * 5,
        out_specs=[in_hbm] * 4,
        scratch_shapes=[space(*whole3)] * 3
        + [space(nx // 8, ny // 8, LANES // 2), pltpu.SemaphoreType.DMA((16,))],
        compiler_params=pltpu.CompilerParams(vmem_limit_bytes=4 * 2**20),
        name="results",
    )(*[pltpu.with_memory_space_constraint(x, pltpu.VMEM) for x in fields])


def solution(mesh):
    spec = P("gx", "gy", None)
    counts = (mesh.shape["gx"], mesh.shape["gy"])
    return jax.shard_map(
        functools.partial(body, counts),
        mesh=mesh,
        in_specs=(spec,) * 5,
        out_specs=(spec,) * 4,
        check_vma=False,
    )
```

```python
import functools

import jax
import jax.numpy as jnp
from jax import lax
from jax.experimental import pallas as pl
from jax.experimental.pallas import tpu as pltpu
from jax.sharding import PartitionSpec as P

DEGREE = 4
CHEB_HIGH = 2.0
CHEB_LOW = 0.25
LANES = 128
PAD = 8
REACH = 4
CUTS = (2, 4, 5)
EARLY = 1
COPIES = 96
MESH = pl.DeviceIdType.MESH
F32 = jnp.float32
BF16 = jnp.bfloat16


def chebyshev_weights():
    theta = 0.5 * (CHEB_HIGH + CHEB_LOW)
    delta = 0.5 * (CHEB_HIGH - CHEB_LOW)
    sigma = theta / delta
    old = 1.0 / sigma
    first, second = [], []
    for _ in range(1, DEGREE):
        new = 1.0 / (2.0 * sigma - old)
        first.append(new * old)
        second.append(2.0 * new / delta)
        old = new
    s1 = 1.0 / theta
    s2 = second[0] * s1
    s3 = second[1] * s2
    s4 = second[2] * s3
    keep = [1.0 + first[k] - second[k] for k in range(3)]
    return (
        (((keep[0] * s1 + second[0]) / s2,), 1.0),
        ((keep[1] * s2 / s3, (second[1] - first[1] * s1) / s3), 1.0),
        ((keep[2] * s3, -first[2] * s2, second[2]), s4),
    )


WEIGHTS = chebyshev_weights()


def loop(low, high, step, fn):
    turns = (high - low) // step

    def turn(i, _):
        fn(low + i * step, step)
        return 0

    if turns == 1:
        fn(low, step)
    elif turns:
        lax.fori_loop(0, turns, turn, 0)
    if low + turns * step < high:
        fn(low + turns * step, high - low - turns * step)


def each(fn):
    def block(first, number):
        for k in range(number):
            fn(first + k)

    return block


def lane_index(shape):
    return lax.broadcasted_iota(jnp.int32, shape, len(shape) - 1)


def z_below(v):
    turned = pltpu.roll(v, 1, 2)
    if v.shape[0] == 1:
        return turned
    before = jnp.concatenate([turned[-1:], turned[:-1]], axis=0)
    return jnp.where(lane_index(v.shape) == 0, before, turned)


def z_above(v):
    turned = pltpu.roll(v, LANES - 1, 2)
    if v.shape[0] == 1:
        return turned
    after = jnp.concatenate([turned[1:], turned[:1]], axis=0)
    return jnp.where(lane_index(v.shape) == LANES - 1, after, turned)


def neighbour_sums(u, du, dr, bx, by, bz, p, number, r, size):
    here = pl.ds(r + dr, size)
    before, v, lower = u[p + du - 1, :, here, :], u[p + du, :, here, :], bx(p, r)
    for k in range(number):
        q = p + k
        after, upper = u[q + du + 1, :, here, :], bx(q + 1, r)
        depth = bz(q, r)
        total = lower * before + upper * after
        total = total + by(q, r) * u[q + du, :, pl.ds(r + dr - 1, size), :]
        total = total + by(q, r + 1) * u[q + du, :, pl.ds(r + dr + 1, size), :]
        yield q, v, total + (depth * z_below(v) + z_above(depth * v))
        before, v, lower = v, after, upper


def inverse_of(diag):
    guess = pl.reciprocal(diag, approx=True)
    return guess * (2.0 - diag * guess)


def fold(values, table):
    high = values.astype(BF16)
    low = (values - high.astype(F32)).astype(BF16)
    both = jnp.dot(jnp.concatenate([high, low], axis=0), table, preferred_element_type=F32)
    return both[: values.shape[0]] + both[values.shape[0] :]


def fold_planes(blocks, table):
    tiles, rows, _ = blocks[0].shape
    if tiles == 1:
        stacked = jnp.concatenate([block[0] for block in blocks], axis=0)
        out = fold(stacked, table)
        return [out[i * rows : (i + 1) * rows][None] for i in range(len(blocks))]
    parts = []
    for block in blocks:
        for t in range(0, tiles, 2):
            parts.append(jnp.concatenate([block[t], block[t + 1]], axis=1))
    out = fold(jnp.concatenate(parts, axis=0), table)
    half = tiles // 2
    result = []
    for i in range(len(blocks)):
        rows_of = [out[(i * half + t) * rows : (i * half + t + 1) * rows] for t in range(half)]
        result.append(jnp.stack(rows_of, axis=0))
    return result


def level_dims(dims, level):
    nx, ny, nz = dims
    return nx >> level, ny >> level, max((nz // LANES) >> level, 1)


def reach_of(dims, level):
    return min(REACH, dims[0] >> level)


def combine(weights, v, total, inverse, older):
    factors, scale = weights
    change = inverse * total
    if scale != 1.0:
        change = change * scale
    value = factors[0] * v
    for factor, field in zip(factors[1:], older):
        value = value + factor * field
    return value + change


def wide_sweeps(dims, level, ext, chain, targets):
    planes, rows, count = level_dims(dims, level)
    whole = planes + 2 * reach_of(dims, level)
    step = 6 if level == 1 else whole
    chain = list(chain)
    for k, target in enumerate(targets):
        u, older = chain[0], chain[1:]
        if k == 2 and level == 3:
            first, length = PAD, rows
        else:
            first, length = PAD - REACH, rows + 2 * REACH
        cut = first + (length + 8) // 16 * 8 if count > 1 else first + length

        def sweep(p, number):
            for low, high in ((first, cut), (cut, first + length)):
                if low == high:
                    continue
                place = pl.ds(low, high - low)
                faces = coarse_faces(ext, count, high - low)
                for q, v, total in neighbour_sums(u, 0, 0, *faces, p, number, low, high - low):
                    past = [field[q, :, place, :] for field in older]
                    inverse = ext[q, pl.ds(3 * count, count), place, :]
                    target[q, :, place, :] = combine(WEIGHTS[k], v, total, inverse, past)

        loop(k + 1, whole - k - 1, step, sweep)
        chain.insert(0, target)


def coarse_faces(ext, count, length):
    def face(a):
        return lambda p, r: ext[p, pl.ds(a * count, count), pl.ds(r, length), :]

    return face(0), face(1), face(2)


def kernel(dims, counts, *refs):
    nx, ny, nz = dims
    tiles = nz // LANES
    refs = list(refs)
    rhs_h, alpha_h, bx_h, by_h, bz_h = refs[:5]
    u4, mid, low, ext3, first3 = refs[5:10]
    f0, al0, bx0, by0, bz0, inv0, diag0, u1, u2, u3 = refs[10:20]
    rt = al0
    table_pair, table_even, small_pair, small_even = refs[20:24]
    coarse = [refs[24:34] + [mid], refs[34:44] + [low], refs[44:49] + [ext3, None, first3]]
    in_sem, send_sem, recv_sem = refs[49:52]

    gx, gy = lax.axis_index("gx"), lax.axis_index("gy")
    cx, cy = counts

    def device(ox, oy):
        return (lax.rem(gx + ox + cx, cx), lax.rem(gy + oy + cy, cy))

    around = [(ox, oy) for ox in (-1, 0, 1) for oy in (-1, 0, 1) if (ox, oy) != (0, 0)]

    used = [0]
    sent = []

    def send(src, dst, where):
        index = used[0]
        used[0] += 1
        copy = pltpu.make_async_remote_copy(
            src_ref=src,
            dst_ref=dst,
            send_sem=send_sem.at[index],
            recv_sem=recv_sem.at[index],
            device_id=device(*where),
            device_id_type=MESH,
        )
        copy.start()
        sent.append(copy)
        return copy

    locals_of = ((bx_h, bx0), (by_h, by0), (bz_h, bz0), (alpha_h, al0), (rhs_h, f0))
    edge = 8
    cuts = [2] + [nx * k // 6 for k in CUTS] + [nx - 2]

    def pieces(a):
        more_rows, more_planes = (edge if a == 1 else 0), (1 if a == 0 else 0)
        low, low2, top, top2 = edge + more_rows, 2 * edge + more_rows, ny - edge, ny - 2 * edge
        one, two = 1 + more_planes, 2 + more_planes
        parts = [((0, nx), (0, low)), ((0, nx), (top, ny)), ((0, one), (low, top)), ((nx - 1, nx), (low, top))]
        parts += [((one, nx - 1), (low, low2)), ((one, nx - 1), (top2, top))]
        parts += [((one, two), (low2, top2)), ((nx - 2, nx - 1), (low2, top2))]
        for g in range(len(cuts) - 1):
            parts.append(((max(cuts[g], two), cuts[g + 1]), (low2, top2)))
        return parts

    def part_of(ref, planes, rows):
        return ref.at[pl.ds(planes[0], planes[1] - planes[0]), :, pl.ds(rows[0], rows[1] - rows[0])]

    def load(n):
        for a, (src, dst) in enumerate(locals_of):
            planes, rows = pieces(a)[n]
            for t in range(tiles):
                pltpu.make_async_copy(
                    part_of(src, planes, (t * LANES, (t + 1) * LANES)).at[:, pl.ds(rows[0], rows[1] - rows[0])],
                    part_of(dst, planes, rows).at[:, t],
                    in_sem.at[a, n],
                ).start()

    def wait_input(n):
        for a, (_, dst) in enumerate(locals_of):
            part = part_of(dst, *pieces(a)[n])
            pltpu.make_async_copy(part, part, in_sem.at[a, n]).wait()

    barrier = pltpu.get_barrier_semaphore()
    for where in around:
        pl.semaphore_signal(barrier, inc=1, device_id=device(*where), device_id_type=MESH)
    for n in range(4):
        load(n)

    def fill(ref, even):
        k = lax.broadcasted_iota(jnp.int32, ref.shape, 0)
        c = lax.broadcasted_iota(jnp.int32, ref.shape, 1)
        if ref.shape[0] == LANES:
            c = c % (LANES // 2)
        hit = k == 2 * c if even else k // 2 == c
        ref[...] = jnp.where(hit, 1.0, 0.0).astype(BF16)

    fill(table_pair, False)
    fill(table_even, True)
    fill(small_pair, False)
    fill(small_even, True)

    pl.semaphore_wait(barrier, len(around))

    halo = []
    for t in range(tiles):
        lanes = pl.ds(t * LANES, LANES)
        halo.append(send(by_h.at[:, pl.ds(0, 1), lanes], by0.at[:, t, pl.ds(ny, 1)], (0, -1)))
    for t in range(tiles):
        lanes = pl.ds(t * LANES, LANES)
        halo.append(send(bx_h.at[0, :, lanes], bx0.at[nx, t], (-1, 0)))

    for n in range(4, 7 + len(cuts)):
        load(n)

    def start_rows(p, r, size):
        rows = pl.ds(r, size)
        depth = bz0[p, :, rows, :]
        diag = al0[p, :, rows, :] + bx0[p, :, rows, :] + bx0[p + 1, :, rows, :]
        diag = diag + by0[p, :, rows, :] + by0[p, :, pl.ds(r + 1, size), :]
        diag = diag + depth + z_above(depth)
        inverse = inverse_of(diag)
        diag0[p, :, rows, :] = diag
        inv0[p, :, rows, :] = inverse
        u1[p + 1, :, pl.ds(r + PAD, size), :] = inverse * f0[p, :, rows, :]

    def start_ends(j):
        r = pl.multiple_of(j * 16, 16)
        start_rows(0, r, 16)
        start_rows(nx - 1, r, 16)

    def start_edges(p):
        start_rows(p, 0, 8)
        start_rows(p, ny - 8, 8)

    def start_next(p):
        start_rows(p, edge, edge)
        start_rows(p, ny - 2 * edge, edge)

    def start_inner(p):
        for r in range(2 * edge, ny - 2 * edge, 16):
            start_rows(p, r, 16)

    def send_planes(u):
        rows = pl.ds(PAD, ny)
        return [
            send(u.at[1, :, rows], u.at[nx + 1, :, rows], (-1, 0)),
            send(u.at[nx, :, rows], u.at[0, :, rows], (1, 0)),
        ]

    def send_rows(u):
        planes = pl.ds(1, nx)
        return [
            send(u.at[planes, :, pl.ds(PAD, 1)], u.at[planes, :, pl.ds(PAD + ny, 1)], (0, -1)),
            send(u.at[planes, :, pl.ds(PAD + ny - 1, 1)], u.at[planes, :, pl.ds(PAD - 1, 1)], (0, 1)),
        ]

    def land(copies):
        for copy in copies:
            copy.wait_recv()

    def pair_rows(ref, p, size):
        return ref[p, :, pl.ds(0, size, 2), :] + ref[p, :, pl.ds(1, size, 2), :]

    def restrict_block(level, source, table_p, table_e, plane_list, with_x):
        al, bx, by, bz = source
        al_c, bx_c, by_c, bz_c = coarse[level - 1][:4]
        rows = ny >> level
        more = rows + PAD
        planes = plane_list
        folded = fold_planes([pair_rows(bx, 2 * p, rows) for p in planes], table_p)
        for p, value in zip(planes, folded):
            bx_c[p, :, pl.ds(0, rows), :] = value * 0.0625
        if not with_x:
            return
        folded = fold_planes(
            [by[2 * p, :, pl.ds(0, more, 2), :] + by[2 * p + 1, :, pl.ds(0, more, 2), :] for p in planes], table_p
        )
        for p, value in zip(planes, folded):
            by_c[p, :, pl.ds(0, more), :] = value * 0.0625
        folded = fold_planes([pair_rows(bz, 2 * p, rows) + pair_rows(bz, 2 * p + 1, rows) for p in planes], table_e)
        for p, value in zip(planes, folded):
            bz_c[p, :, pl.ds(0, rows), :] = value * 0.0625
        folded = fold_planes([pair_rows(al, 2 * p, rows) + pair_rows(al, 2 * p + 1, rows) for p in planes], table_p)
        for p, value in zip(planes, folded):
            al_c[p, :, pl.ds(0, rows), :] = value * 0.125

    def coarse_plane(level, p):
        al, bx, by, bz, diag_c, ext = coarse[level - 1][:6]
        _, rows, count = level_dims(dims, level)
        reach = reach_of(dims, level)
        own = pl.ds(0, rows)
        lower_x, lower_y, depth = bx[p, :, own, :], by[p, :, own, :], bz[p, :, own, :]
        diag = al[p, :, own, :] + lower_x + bx[p + 1, :, own, :]
        diag = diag + lower_y + by[p, :, pl.ds(1, rows), :] + depth + z_above(depth)
        diag_c[p, :, :, :] = diag
        place = pl.ds(PAD, rows)
        for a, value in enumerate((lower_x, lower_y, depth, inverse_of(diag))):
            ext[p + reach, pl.ds(a * count, count), place, :] = value

    def send_outer(field, level, ox, oy, part, below=REACH, above=REACH):
        planes, rows, _ = level_dims(dims, level)
        reach = reach_of(dims, level)
        depth = {-1: min(below, reach), 0: planes, 1: min(above, reach)}[ox]
        width = {-1: below, 0: rows, 1: above}[oy]
        from_x = {-1: reach, 0: reach, 1: reach + planes - depth}[ox]
        to_x = {-1: reach + planes, 0: reach, 1: reach - depth}[ox]
        from_y = {-1: PAD, 0: PAD, 1: PAD + rows - width}[oy]
        to_y = {-1: PAD + rows, 0: PAD, 1: PAD - width}[oy]
        return send(
            field.at[pl.ds(from_x, depth), part, pl.ds(from_y, width)],
            field.at[pl.ds(to_x, depth), part, pl.ds(to_y, width)],
            (ox, oy),
        )

    sides = [where for where in around if 0 in where]
    corners = [where for where in around if 0 not in where]

    def send_wide(level, places, arrays, below=REACH, above=REACH - 1):
        count = level_dims(dims, level)[2]
        part = pl.ds(arrays[0] * count, (arrays[1] - arrays[0]) * count)
        return [send_outer(coarse[level - 1][5], level, ox, oy, part, below, above) for ox, oy in places]

    def send_source(level, ox):
        part = pl.ds(0, level_dims(dims, level)[2])
        field = coarse[level - 1][7]
        return [send_outer(field, level, ox, oy, part) for oy in (-1, 1, 0) if (ox, oy) != (0, 0)]

    fine_coeffs = (al0, bx0, by0, bz0)

    def first_coarse(p):
        restrict_block(1, fine_coeffs, table_pair[...], table_even[...], [2 * p, 2 * p + 1], True)

    def first_plane(p):
        coarse_plane(1, p)

    def lower_coarse():
        for level in (2, 3):
            tables = (table_pair, table_even) if level == 2 else (small_pair, small_even)
            planes = nx >> level
            source = coarse[level - 2][:4]
            restrict_block(level, source, tables[0][...], tables[1][...], list(range(planes)), True)
            restrict_block(level, source, tables[0][...], tables[1][...], [planes], False)
            for p in range(planes):
                coarse_plane(level, p)

    def fine_face(ref, size):
        return lambda p, r: ref[p, :, pl.ds(r, size), :]

    def fine_sums(u, p, number, r, size):
        faces = fine_face(bx0, size), fine_face(by0, size), fine_face(bz0, size)
        return neighbour_sums(u, 1, PAD, *faces, p, number, r, size)

    def fine_sweep(weights, fields, target):
        u, older = fields[0], fields[1:]

        def update(p, number, r, size):
            place = pl.ds(r + PAD, size)
            for q, v, total in fine_sums(u, p, number, r, size):
                past = [field[q + 1, :, place, :] for field in older]
                inverse = inv0[q, :, pl.ds(r, size), :]
                target[q + 1, :, place, :] = combine(weights, v, total, inverse, past)

        def end_planes(j):
            r = pl.multiple_of(j * 16, 16)
            update(0, 1, r, 16)
            update(nx - 1, 1, r, 16)

        def end_rows(p, number):
            update(p, number, 0, 8)
            update(p, number, ny - 8, 8)

        def inner(p, number):
            for r in range(8, ny - 8, 8):
                update(p, number, r, 8)

        def outer():
            loop(0, ny // 16, 2, each(end_planes))
            copies = send_planes(target)
            loop(1, nx - 1, 4, end_rows)
            return copies + send_rows(target)

        return outer, lambda: loop(1, nx - 1, 4, inner)

    sweeps = [fine_sweep(WEIGHTS[k], (u3, u2, u1)[2 - k :], (u2, u3, u4)[k]) for k in range(3)]

    for n in range(4):
        wait_input(n)
    land(halo)
    loop(0, ny // 16, 2, each(start_ends))
    flying = send_planes(u1)
    loop(1, nx - 1, 4, each(start_edges))
    flying += send_rows(u1)
    restrict_block(1, fine_coeffs, table_pair[...], table_even[...], [nx // 2], False)
    for n in range(4, 8):
        wait_input(n)
    loop(1, nx - 1, 4, each(start_next))
    start_inner(1)
    start_inner(nx - 2)
    done = 0
    for g in range(len(cuts) - 1):
        wait_input(8 + g)
        final = g == len(cuts) - 2
        loop(max(cuts[g] - 1, 2), nx - 2 if final else cuts[g + 1] - 1, 2, each(start_inner))
        ready = nx // 4 if final else cuts[g + 1] // 4
        loop(done, ready, 1, each(first_coarse))
        done = ready
        if g == EARLY:
            land(flying)
            flying = sweeps[0][0]()
    loop(0, nx // 2, 4, each(first_plane))
    wide = send_wide(1, sides, (0, 2))
    sweeps[0][1]()
    lower_coarse()
    for k in (1, 2):
        land(flying)
        flying = sweeps[k][0]()
        if k == 1:
            wide += send_wide(1, sides, (2, 4), REACH - 1) + send_wide(1, corners, (0, 4))
        else:
            wide += send_wide(2, around, (0, 4)) + send_wide(3, around, (0, 4))
        sweeps[k][1]()

    def residual_rows(p, number, rows):
        for r in rows:
            own = pl.ds(r, 8)
            kept = None
            for q, v, total in fine_sums(u4, 2 * p, 2 * number, r, 8):
                value = f0[q, :, own, :] - diag0[q, :, own, :] * v + total
                if kept is None:
                    kept = q, value
                else:
                    rt[kept[0] // 2, :, own, :] = kept[1] + value
                    kept = None

    def residual_whole(j):
        r = pl.multiple_of(j * 8, 8)
        residual_rows(0, 1, [r])
        residual_rows(nx // 2 - 1, 1, [r])

    def residual_edges(p, number):
        residual_rows(p, number, (0, ny - 8))

    def residual_inner(p, number):
        residual_rows(p, number, range(8, ny - 8, 8))

    loop(1, nx // 2 - 1, 2, residual_inner)
    land(flying)
    loop(0, ny // 8, 2, each(residual_whole))

    def put_source(level, p, value):
        _, rows, count = level_dims(dims, level)
        ext, source, first = coarse[level - 1][5:8]
        q = p + reach_of(dims, level)
        own = pl.ds(PAD, rows)
        value = value * 0.125
        if source is not None:
            source[p] = value
        first[q, :, own, :] = ext[q, pl.ds(3 * count, count), own, :] * value

    def first_source(low):
        planes = range(low, low + REACH)
        folded = fold_planes([pair_rows(rt, p, ny // 2) for p in planes], table_pair[...])
        for p, value in zip(planes, folded):
            put_source(1, p, value)

    flying = []
    half = nx // 2
    for low_p, ox in ((0, -1), (half - REACH, 1)):
        first, last = max(low_p, 1), min(low_p + REACH, half - 1)
        residual_edges(first, last - first)
        first_source(low_p)
        flying += send_source(1, ox)
    loop(REACH, half - REACH, REACH, residual_edges)
    for low_p in range(REACH, half - REACH, REACH):
        first_source(low_p)
    flying += send_source(1, 0)

    land(wide)
    for level in (1, 2):
        land(flying)
        diag_c, ext, source, c1, c2, c3, c4 = coarse[level - 1][4:11]
        wide_sweeps(dims, level, ext, [c1], (c2, c3, c4))
        planes, rows, count = level_dims(dims, level)
        reach = reach_of(dims, level)
        faces = coarse_faces(ext, count, rows)

        def pair(p, number):
            kept = None
            for q, v, total in neighbour_sums(c4, 0, 0, *faces, 2 * p + reach, 2 * number, PAD, rows):
                value = source[q - reach] - diag_c[q - reach] * v + total
                if kept is None:
                    kept = value
                else:
                    c2[(q - reach) // 2, :, pl.ds(0, rows), :] = kept + value
                    kept = None

        loop(0, planes // 2, 3, pair)
        table = table_pair if level == 1 else small_pair
        folded = fold_planes([pair_rows(c2, p, rows // 2) for p in range(planes // 2)], table[...])
        for p, value in enumerate(folded):
            put_source(level + 1, p, value)
        flying = send_source(level + 1, -1) + send_source(level + 1, 1) + send_source(level + 1, 0)
    land(flying)
    for copy in sent:
        copy.wait_send()


def last_kernel(dims, u4, mid, low, ext3, first3, *refs):
    outs, (c2, c3, c4, top, sem) = refs[:4], refs[4:]
    stores = []
    for level, field in enumerate((u4, mid, low)):
        planes, rows, count = level_dims(dims, level)
        own = pl.ds(reach_of(dims, level) if level else 1, planes)
        for t in range(count):
            copy = pltpu.make_async_copy(
                field.at[own, t, pl.ds(PAD, rows)],
                outs[level].at[:, :, pl.ds(t * LANES, LANES)],
                sem.at[len(stores)],
            )
            copy.start()
            stores.append(copy)
    wide_sweeps(dims, 3, ext3, [first3], (c2, c3, c4))
    planes, rows, _ = level_dims(dims, 3)
    top[...] = c4[pl.ds(reach_of(dims, 3), planes), 0, pl.ds(PAD, rows), pl.ds(0, LANES // 2)]
    copy = pltpu.make_async_copy(top, outs[3], sem.at[len(stores)])
    copy.start()
    for store in stores + [copy]:
        store.wait()


def space(*shape):
    return pltpu.VMEM(shape, F32)


def halo_shape(dims, level):
    x, y, t = level_dims(dims, level)
    around = reach_of(dims, level) if level else 1
    return (x + 2 * around, t, y + 2 * PAD, LANES)


def scratch_of(dims):
    nx, ny, nz = dims
    tiles = nz // LANES
    shapes = [
        space(nx, tiles, ny, LANES),
        space(nx, tiles, ny, LANES),
        space(nx + 1, tiles, ny, LANES),
        space(nx, tiles, ny + 2 * PAD, LANES),
        space(nx, tiles, ny, LANES),
        space(nx, tiles, ny, LANES),
        space(nx, tiles, ny, LANES),
    ]
    shapes += [space(*halo_shape(dims, 0))] * 3
    shapes += [pltpu.VMEM((2 * LANES, LANES), BF16)] * 2
    shapes += [pltpu.VMEM((LANES, LANES), BF16)] * 2
    for level in (1, 2, 3):
        x, y, t = level_dims(dims, level)
        tall = y + 2 * PAD
        shapes += [
            space(x, t, y, LANES),
            space(x + 1, t, y, LANES),
            space(x, t, tall, LANES),
            space(x, t, y, LANES),
            space(x, t, y, LANES),
        ]
        if level < 3:
            whole = halo_shape(dims, level)
            shapes += [space(whole[0], 4 * t, tall, LANES), space(x, t, y, LANES)]
            shapes += [space(*whole)] * 3
    shapes += [
        pltpu.SemaphoreType.DMA((5, 9 + len(CUTS))),
        pltpu.SemaphoreType.DMA((COPIES,)),
        pltpu.SemaphoreType.DMA((COPIES,)),
    ]
    return shapes


def body(counts, *args):
    dims = args[0].shape
    nx, ny, nz = dims
    whole3 = halo_shape(dims, 3)
    kept = [halo_shape(dims, level) for level in range(3)]
    kept += [(whole3[0], 4) + whole3[2:], whole3]
    in_hbm = pl.BlockSpec(memory_space=pltpu.HBM)
    in_vmem = pl.BlockSpec(memory_space=pltpu.VMEM)
    fields = pl.pallas_call(
        functools.partial(kernel, dims, counts),
        out_shape=[pltpu.VMEM(shape, F32) for shape in kept],
        in_specs=[in_hbm] * 5,
        out_specs=[in_vmem] * 5,
        scratch_shapes=scratch_of(dims),
        compiler_params=pltpu.CompilerParams(
            collective_id=0, has_side_effects=True, vmem_limit_bytes=48 * 2**20
        ),
        name="sweep",
    )(*[pltpu.with_memory_space_constraint(x, pltpu.HBM) for x in args])
    return pl.pallas_call(
        functools.partial(last_kernel, dims),
        out_shape=[pltpu.HBM((nx >> k, ny >> k, nz >> k), F32) for k in range(4)],
        in_specs=[in_vmem] * 5,
        out_specs=[in_hbm] * 4,
        scratch_shapes=[space(*whole3)] * 3
        + [space(nx // 8, ny // 8, LANES // 2), pltpu.SemaphoreType.DMA((16,))],
        compiler_params=pltpu.CompilerParams(vmem_limit_bytes=4 * 2**20),
        name="results",
    )(*[pltpu.with_memory_space_constraint(x, pltpu.VMEM) for x in fields])


def solution(mesh):
    spec = P("gx", "gy", None)
    counts = (mesh.shape["gx"], mesh.shape["gy"])
    return jax.shard_map(
        functools.partial(body, counts),
        mesh=mesh,
        in_specs=(spec,) * 5,
        out_specs=(spec,) * 4,
        check_vma=False,
    )
```

```python
import functools

import jax
import jax.numpy as jnp
from jax import lax
from jax.experimental import pallas as pl
from jax.experimental.pallas import tpu as pltpu
from jax.sharding import PartitionSpec as P

DEGREE = 4
CHEB_HIGH = 2.0
CHEB_LOW = 0.25
LANES = 128
PAD = 8
REACH = 4
CUTS = (2, 4, 5)
EARLY = 1
COPIES = 96
MESH = pl.DeviceIdType.MESH
F32 = jnp.float32
BF16 = jnp.bfloat16


def chebyshev_weights():
    theta = 0.5 * (CHEB_HIGH + CHEB_LOW)
    delta = 0.5 * (CHEB_HIGH - CHEB_LOW)
    sigma = theta / delta
    old = 1.0 / sigma
    first, second = [], []
    for _ in range(1, DEGREE):
        new = 1.0 / (2.0 * sigma - old)
        first.append(new * old)
        second.append(2.0 * new / delta)
        old = new
    s1 = 1.0 / theta
    s2 = second[0] * s1
    s3 = second[1] * s2
    s4 = second[2] * s3
    keep = [1.0 + first[k] - second[k] for k in range(3)]
    return (
        (((keep[0] * s1 + second[0]) / s2,), 1.0),
        ((keep[1] * s2 / s3, (second[1] - first[1] * s1) / s3), 1.0),
        ((keep[2] * s3, -first[2] * s2, second[2]), s4),
    )


WEIGHTS = chebyshev_weights()


def loop(low, high, step, fn):
    turns = (high - low) // step

    def turn(i, _):
        fn(low + i * step, step)
        return 0

    if turns == 1:
        fn(low, step)
    elif turns:
        lax.fori_loop(0, turns, turn, 0)
    if low + turns * step < high:
        fn(low + turns * step, high - low - turns * step)


def each(fn):
    def block(first, number):
        for k in range(number):
            fn(first + k)

    return block


def lane_index(shape):
    return lax.broadcasted_iota(jnp.int32, shape, len(shape) - 1)


def z_below(v):
    turned = pltpu.roll(v, 1, 2)
    if v.shape[0] == 1:
        return turned
    before = jnp.concatenate([turned[-1:], turned[:-1]], axis=0)
    return jnp.where(lane_index(v.shape) == 0, before, turned)


def z_above(v):
    turned = pltpu.roll(v, LANES - 1, 2)
    if v.shape[0] == 1:
        return turned
    after = jnp.concatenate([turned[1:], turned[:1]], axis=0)
    return jnp.where(lane_index(v.shape) == LANES - 1, after, turned)


def neighbour_sums(u, du, dr, bx, by, bz, p, number, r, size):
    here = pl.ds(r + dr, size)
    before, v, lower = u[p + du - 1, :, here, :], u[p + du, :, here, :], bx(p, r)
    for k in range(number):
        q = p + k
        after, upper = u[q + du + 1, :, here, :], bx(q + 1, r)
        depth = bz(q, r)
        total = lower * before + upper * after
        total = total + by(q, r) * u[q + du, :, pl.ds(r + dr - 1, size), :]
        total = total + by(q, r + 1) * u[q + du, :, pl.ds(r + dr + 1, size), :]
        yield q, v, total + (depth * z_below(v) + z_above(depth * v))
        before, v, lower = v, after, upper


def inverse_of(diag):
    guess = pl.reciprocal(diag, approx=True)
    return guess * (2.0 - diag * guess)


def fold(values, table):
    high = values.astype(BF16)
    low = (values - high.astype(F32)).astype(BF16)
    both = jnp.dot(jnp.concatenate([high, low], axis=0), table, preferred_element_type=F32)
    return both[: values.shape[0]] + both[values.shape[0] :]


def fold_planes(blocks, table):
    tiles, rows, _ = blocks[0].shape
    if tiles == 1:
        stacked = jnp.concatenate([block[0] for block in blocks], axis=0)
        out = fold(stacked, table)
        return [out[i * rows : (i + 1) * rows][None] for i in range(len(blocks))]
    parts = []
    for block in blocks:
        for t in range(0, tiles, 2):
            parts.append(jnp.concatenate([block[t], block[t + 1]], axis=1))
    out = fold(jnp.concatenate(parts, axis=0), table)
    half = tiles // 2
    result = []
    for i in range(len(blocks)):
        rows_of = [out[(i * half + t) * rows : (i * half + t + 1) * rows] for t in range(half)]
        result.append(jnp.stack(rows_of, axis=0))
    return result


def level_dims(dims, level):
    nx, ny, nz = dims
    return nx >> level, ny >> level, max((nz // LANES) >> level, 1)


def reach_of(dims, level):
    return min(REACH, dims[0] >> level)


def combine(weights, v, total, inverse, older):
    factors, scale = weights
    change = inverse * total
    if scale != 1.0:
        change = change * scale
    value = factors[0] * v
    for factor, field in zip(factors[1:], older):
        value = value + factor * field
    return value + change


def wide_sweeps(dims, level, ext, chain, targets):
    planes, rows, count = level_dims(dims, level)
    whole = planes + 2 * reach_of(dims, level)
    step = 6 if level == 1 else whole
    chain = list(chain)
    for k, target in enumerate(targets):
        u, older = chain[0], chain[1:]
        if k == 2 and level == 3:
            first, length = PAD, rows
        else:
            first, length = PAD - REACH, rows + 2 * REACH
        cut = first + (length + 8) // 16 * 8 if count > 1 else first + length

        def sweep(p, number):
            for low, high in ((first, cut), (cut, first + length)):
                if low == high:
                    continue
                place = pl.ds(low, high - low)
                faces = coarse_faces(ext, count, high - low)
                for q, v, total in neighbour_sums(u, 0, 0, *faces, p, number, low, high - low):
                    past = [field[q, :, place, :] for field in older]
                    inverse = ext[q, pl.ds(3 * count, count), place, :]
                    target[q, :, place, :] = combine(WEIGHTS[k], v, total, inverse, past)

        loop(k + 1, whole - k - 1, step, sweep)
        chain.insert(0, target)


def coarse_faces(ext, count, length):
    def face(a):
        return lambda p, r: ext[p, pl.ds(a * count, count), pl.ds(r, length), :]

    return face(0), face(1), face(2)


def kernel(dims, counts, *refs):
    nx, ny, nz = dims
    tiles = nz // LANES
    refs = list(refs)
    rhs_h, alpha_h, bx_h, by_h, bz_h = refs[:5]
    u4, mid, low, ext3, first3 = refs[5:10]
    f0, al0, bx0, by0, bz0, inv0, diag0, u1, u2, u3 = refs[10:20]
    rt = al0
    table_pair, table_even, small_pair, small_even = refs[20:24]
    coarse = [refs[24:34] + [mid], refs[34:44] + [low], refs[44:49] + [ext3, None, first3]]
    in_sem, send_sem, recv_sem = refs[49:52]

    gx, gy = lax.axis_index("gx"), lax.axis_index("gy")
    cx, cy = counts

    def device(ox, oy):
        return (lax.rem(gx + ox + cx, cx), lax.rem(gy + oy + cy, cy))

    around = [(ox, oy) for ox in (-1, 0, 1) for oy in (-1, 0, 1) if (ox, oy) != (0, 0)]

    used = [0]
    sent = []

    def send(src, dst, where):
        index = used[0]
        used[0] += 1
        copy = pltpu.make_async_remote_copy(
            src_ref=src,
            dst_ref=dst,
            send_sem=send_sem.at[index],
            recv_sem=recv_sem.at[index],
            device_id=device(*where),
            device_id_type=MESH,
        )
        copy.start()
        sent.append(copy)
        return copy

    locals_of = ((bx_h, bx0), (by_h, by0), (bz_h, bz0), (alpha_h, al0), (rhs_h, f0))
    edge = 8
    cuts = [2] + [nx * k // 6 for k in CUTS] + [nx - 2]

    def pieces(a):
        more_rows, more_planes = (edge if a == 1 else 0), (1 if a == 0 else 0)
        low, low2, top, top2 = edge + more_rows, 2 * edge + more_rows, ny - edge, ny - 2 * edge
        one, two = 1 + more_planes, 2 + more_planes
        parts = [((0, nx), (0, low)), ((0, nx), (top, ny)), ((0, one), (low, top)), ((nx - 1, nx), (low, top))]
        parts += [((one, nx - 1), (low, low2)), ((one, nx - 1), (top2, top))]
        parts += [((one, two), (low2, top2)), ((nx - 2, nx - 1), (low2, top2))]
        for g in range(len(cuts) - 1):
            parts.append(((max(cuts[g], two), cuts[g + 1]), (low2, top2)))
        return parts

    def part_of(ref, planes, rows):
        return ref.at[pl.ds(planes[0], planes[1] - planes[0]), :, pl.ds(rows[0], rows[1] - rows[0])]

    def load(n):
        for a, (src, dst) in enumerate(locals_of):
            planes, rows = pieces(a)[n]
            for t in range(tiles):
                pltpu.make_async_copy(
                    part_of(src, planes, (t * LANES, (t + 1) * LANES)).at[:, pl.ds(rows[0], rows[1] - rows[0])],
                    part_of(dst, planes, rows).at[:, t],
                    in_sem.at[a, n],
                ).start()

    def wait_input(n):
        for a, (_, dst) in enumerate(locals_of):
            part = part_of(dst, *pieces(a)[n])
            pltpu.make_async_copy(part, part, in_sem.at[a, n]).wait()

    barrier = pltpu.get_barrier_semaphore()
    for where in around:
        pl.semaphore_signal(barrier, inc=1, device_id=device(*where), device_id_type=MESH)
    for n in range(4):
        load(n)

    def fill(ref, even):
        k = lax.broadcasted_iota(jnp.int32, ref.shape, 0)
        c = lax.broadcasted_iota(jnp.int32, ref.shape, 1)
        if ref.shape[0] == LANES:
            c = c % (LANES // 2)
        hit = k == 2 * c if even else k // 2 == c
        ref[...] = jnp.where(hit, 1.0, 0.0).astype(BF16)

    fill(table_pair, False)
    fill(table_even, True)
    fill(small_pair, False)
    fill(small_even, True)

    pl.semaphore_wait(barrier, len(around))

    halo = []
    for t in range(tiles):
        lanes = pl.ds(t * LANES, LANES)
        halo.append(send(by_h.at[:, pl.ds(0, 1), lanes], by0.at[:, t, pl.ds(ny, 1)], (0, -1)))
    for t in range(tiles):
        lanes = pl.ds(t * LANES, LANES)
        halo.append(send(bx_h.at[0, :, lanes], bx0.at[nx, t], (-1, 0)))

    for n in range(4, 7 + len(cuts)):
        load(n)

    def start_rows(p, r, size):
        rows = pl.ds(r, size)
        depth = bz0[p, :, rows, :]
        diag = al0[p, :, rows, :] + bx0[p, :, rows, :] + bx0[p + 1, :, rows, :]
        diag = diag + by0[p, :, rows, :] + by0[p, :, pl.ds(r + 1, size), :]
        diag = diag + depth + z_above(depth)
        inverse = inverse_of(diag)
        diag0[p, :, rows, :] = diag
        inv0[p, :, rows, :] = inverse
        u1[p + 1, :, pl.ds(r + PAD, size), :] = inverse * f0[p, :, rows, :]

    def start_ends(j):
        r = pl.multiple_of(j * 16, 16)
        start_rows(0, r, 16)
        start_rows(nx - 1, r, 16)

    def start_edges(p):
        start_rows(p, 0, 8)
        start_rows(p, ny - 8, 8)

    def start_next(p):
        start_rows(p, edge, edge)
        start_rows(p, ny - 2 * edge, edge)

    def start_inner(p):
        for r in range(2 * edge, ny - 2 * edge, 16):
            start_rows(p, r, 16)

    def send_planes(u):
        rows = pl.ds(PAD, ny)
        return [
            send(u.at[1, :, rows], u.at[nx + 1, :, rows], (-1, 0)),
            send(u.at[nx, :, rows], u.at[0, :, rows], (1, 0)),
        ]

    def send_rows(u):
        planes = pl.ds(1, nx)
        return [
            send(u.at[planes, :, pl.ds(PAD, 1)], u.at[planes, :, pl.ds(PAD + ny, 1)], (0, -1)),
            send(u.at[planes, :, pl.ds(PAD + ny - 1, 1)], u.at[planes, :, pl.ds(PAD - 1, 1)], (0, 1)),
        ]

    def land(copies):
        for copy in copies:
            copy.wait_recv()

    def pair_rows(ref, p, size):
        return ref[p, :, pl.ds(0, size, 2), :] + ref[p, :, pl.ds(1, size, 2), :]

    def restrict_block(level, source, table_p, table_e, plane_list, with_x):
        al, bx, by, bz = source
        al_c, bx_c, by_c, bz_c = coarse[level - 1][:4]
        rows = ny >> level
        more = rows + PAD
        planes = plane_list
        folded = fold_planes([pair_rows(bx, 2 * p, rows) for p in planes], table_p)
        for p, value in zip(planes, folded):
            bx_c[p, :, pl.ds(0, rows), :] = value * 0.0625
        if not with_x:
            return
        folded = fold_planes(
            [by[2 * p, :, pl.ds(0, more, 2), :] + by[2 * p + 1, :, pl.ds(0, more, 2), :] for p in planes], table_p
        )
        for p, value in zip(planes, folded):
            by_c[p, :, pl.ds(0, more), :] = value * 0.0625
        folded = fold_planes([pair_rows(bz, 2 * p, rows) + pair_rows(bz, 2 * p + 1, rows) for p in planes], table_e)
        for p, value in zip(planes, folded):
            bz_c[p, :, pl.ds(0, rows), :] = value * 0.0625
        folded = fold_planes([pair_rows(al, 2 * p, rows) + pair_rows(al, 2 * p + 1, rows) for p in planes], table_p)
        for p, value in zip(planes, folded):
            al_c[p, :, pl.ds(0, rows), :] = value * 0.125

    def coarse_plane(level, p):
        al, bx, by, bz, diag_c, ext = coarse[level - 1][:6]
        _, rows, count = level_dims(dims, level)
        reach = reach_of(dims, level)
        own = pl.ds(0, rows)
        lower_x, lower_y, depth = bx[p, :, own, :], by[p, :, own, :], bz[p, :, own, :]
        diag = al[p, :, own, :] + lower_x + bx[p + 1, :, own, :]
        diag = diag + lower_y + by[p, :, pl.ds(1, rows), :] + depth + z_above(depth)
        diag_c[p, :, :, :] = diag
        place = pl.ds(PAD, rows)
        for a, value in enumerate((lower_x, lower_y, depth, inverse_of(diag))):
            ext[p + reach, pl.ds(a * count, count), place, :] = value

    def send_outer(field, level, ox, oy, part, below=REACH, above=REACH):
        planes, rows, _ = level_dims(dims, level)
        reach = reach_of(dims, level)
        depth = {-1: min(below, reach), 0: planes, 1: min(above, reach)}[ox]
        width = {-1: below, 0: rows, 1: above}[oy]
        from_x = {-1: reach, 0: reach, 1: reach + planes - depth}[ox]
        to_x = {-1: reach + planes, 0: reach, 1: reach - depth}[ox]
        from_y = {-1: PAD, 0: PAD, 1: PAD + rows - width}[oy]
        to_y = {-1: PAD + rows, 0: PAD, 1: PAD - width}[oy]
        return send(
            field.at[pl.ds(from_x, depth), part, pl.ds(from_y, width)],
            field.at[pl.ds(to_x, depth), part, pl.ds(to_y, width)],
            (ox, oy),
        )

    sides = [where for where in around if 0 in where]
    corners = [where for where in around if 0 not in where]

    def send_wide(level, places, arrays, below=REACH, above=REACH - 1):
        count = level_dims(dims, level)[2]
        part = pl.ds(arrays[0] * count, (arrays[1] - arrays[0]) * count)
        return [send_outer(coarse[level - 1][5], level, ox, oy, part, below, above) for ox, oy in places]

    def send_source(level, ox):
        part = pl.ds(0, level_dims(dims, level)[2])
        field = coarse[level - 1][7]
        return [send_outer(field, level, ox, oy, part) for oy in (-1, 1, 0) if (ox, oy) != (0, 0)]

    fine_coeffs = (al0, bx0, by0, bz0)

    def first_coarse(p):
        restrict_block(1, fine_coeffs, table_pair[...], table_even[...], [2 * p, 2 * p + 1], True)

    def first_plane(p):
        coarse_plane(1, p)

    def lower_coarse():
        for level in (2, 3):
            tables = (table_pair, table_even) if level == 2 else (small_pair, small_even)
            planes = nx >> level
            source = coarse[level - 2][:4]
            restrict_block(level, source, tables[0][...], tables[1][...], list(range(planes)), True)
            restrict_block(level, source, tables[0][...], tables[1][...], [planes], False)
            for p in range(planes):
                coarse_plane(level, p)

    def fine_face(ref, size):
        return lambda p, r: ref[p, :, pl.ds(r, size), :]

    def fine_sums(u, p, number, r, size):
        faces = fine_face(bx0, size), fine_face(by0, size), fine_face(bz0, size)
        return neighbour_sums(u, 1, PAD, *faces, p, number, r, size)

    def partial_sum(u, q, r, size):
        rows, here = pl.ds(r, size), pl.ds(r + PAD, size)
        v, depth = u[q + 1, :, here, :], bz0[q, :, rows, :]
        total = depth * z_below(v) + z_above(depth * v)
        ends = isinstance(q, int)
        if not (ends and q == 0):
            total = total + bx0[q, :, rows, :] * u[q, :, here, :]
        if not (ends and q == nx - 1):
            total = total + bx0[q + 1, :, rows, :] * u[q + 2, :, here, :]
        row = lax.broadcasted_iota(jnp.int32, v.shape, 1)
        if r == 0:
            below = jnp.where(row == 0, 0.0, pltpu.roll(v, 1, 1))
        else:
            below = u[q + 1, :, pl.ds(r + PAD - 1, size), :]
        if r + size == ny:
            above = jnp.where(row == size - 1, 0.0, pltpu.roll(v, size - 1, 1))
        else:
            above = u[q + 1, :, pl.ds(r + PAD + 1, size), :]
        return v, total + by0[q, :, rows, :] * below + by0[q, :, pl.ds(r + 1, size), :] * above

    def fine_sweep(weights, fields, target):
        u, older = fields[0], fields[1:]

        def update(p, number, r, size):
            place = pl.ds(r + PAD, size)
            for q, v, total in fine_sums(u, p, number, r, size):
                past = [field[q + 1, :, place, :] for field in older]
                inverse = inv0[q, :, pl.ds(r, size), :]
                target[q + 1, :, place, :] = combine(weights, v, total, inverse, past)

        def partly(q, r, size):
            v, total = partial_sum(u, q, r, size)
            rows, here = pl.ds(r, size), pl.ds(r + PAD, size)
            past = [field[q + 1, :, here, :] for field in older]
            target[q + 1, :, here, :] = combine(weights, v, total, inv0[q, :, rows, :], past)

        def mend(q, rows, face, halo):
            change = inv0[q, :, rows, :] * face * halo
            if weights[1] != 1.0:
                change = change * weights[1]
            here = pl.ds(rows.start + PAD, rows.size)
            target[q + 1, :, here, :] = target[q + 1, :, here, :] + change

        def mend_rows(q):
            for row, face, halo in ((0, 0, PAD - 1), (ny - 1, ny, PAD + ny)):
                mend(q, pl.ds(row, 1), by0[q, :, pl.ds(face, 1), :], u[q + 1, :, pl.ds(halo, 1), :])

        def end_rows(q):
            partly(q, 0, 8)
            partly(q, ny - 8, 8)

        def inner(p, number):
            for r in range(8, ny - 8, 8):
                update(p, number, r, 8)

        def before():
            for r in range(0, ny, 16):
                partly(0, r, 16)
                partly(nx - 1, r, 16)
            loop(1, nx - 1, 4, each(end_rows))

        def outer():
            for r in range(0, ny, 16):
                rows, here = pl.ds(r, 16), pl.ds(r + PAD, 16)
                mend(0, rows, bx0[0, :, rows, :], u[0, :, here, :])
                mend(nx - 1, rows, bx0[nx, :, rows, :], u[nx + 1, :, here, :])
            mend_rows(0)
            mend_rows(nx - 1)
            copies = send_planes(target)
            loop(1, nx - 1, 11, each(mend_rows))
            return copies + send_rows(target)

        def deep(p, number):
            for r in range(16, ny - 16, 8):
                update(p, number, r, 8)

        def shell(p, number):
            update(p, number, 8, 8)
            update(p, number, ny - 16, 8)

        def rest():
            loop(1, nx - 1, 4, shell)
            deep(1, 1)
            deep(nx - 2, 1)

        return before, outer, lambda: loop(1, nx - 1, 4, inner), lambda: loop(2, nx - 2, 4, deep), rest


    sweeps = [fine_sweep(WEIGHTS[k], (u3, u2, u1)[2 - k :], (u2, u3, u4)[k]) for k in range(3)]

    for n in range(4):
        wait_input(n)
    land(halo)
    loop(0, ny // 16, 2, each(start_ends))
    flying = send_planes(u1)
    loop(1, nx - 1, 4, each(start_edges))
    flying += send_rows(u1)
    restrict_block(1, fine_coeffs, table_pair[...], table_even[...], [nx // 2], False)
    for n in range(4, 8):
        wait_input(n)
    loop(1, nx - 1, 4, each(start_next))
    start_inner(1)
    start_inner(nx - 2)
    done = 0
    for g in range(len(cuts) - 1):
        wait_input(8 + g)
        final = g == len(cuts) - 2
        loop(max(cuts[g] - 1, 2), nx - 2 if final else cuts[g + 1] - 1, 2, each(start_inner))
        ready = nx // 4 if final else cuts[g + 1] // 4
        loop(done, ready, 1, each(first_coarse))
        done = ready
        if g == EARLY:
            sweeps[0][0]()
            land(flying)
            flying = sweeps[0][1]()
    loop(0, nx // 2, 4, each(first_plane))
    wide = send_wide(1, sides, (0, 2))
    sweeps[0][2]()
    lower_coarse()
    for k in (1, 2):
        sweeps[k][0]()
        land(flying)
        flying = sweeps[k][1]()
        if k == 1:
            wide += send_wide(1, sides, (2, 4), REACH - 1) + send_wide(1, corners, (0, 4))
        else:
            wide += send_wide(2, around, (0, 4)) + send_wide(3, around, (0, 4))
        if k == 1:
            sweeps[1][2]()
            sweeps[2][3]()
        else:
            sweeps[2][4]()

    def residual_rows(p, number, rows):
        for r in rows:
            own = pl.ds(r, 8)
            kept = None
            for q, v, total in fine_sums(u4, 2 * p, 2 * number, r, 8):
                value = f0[q, :, own, :] - diag0[q, :, own, :] * v + total
                if kept is None:
                    kept = q, value
                else:
                    rt[kept[0] // 2, :, own, :] = kept[1] + value
                    kept = None

    def residual_inner(p, number):
        residual_rows(p, number, range(8, ny - 8, 8))

    def residual_partly(p, r, size):
        own = pl.ds(r, size)
        value = 0.0
        for q in (2 * p, 2 * p + 1):
            v, total = partial_sum(u4, q, r, size)
            value = value + (f0[q, :, own, :] - diag0[q, :, own, :] * v + total)
        rt[p, :, own, :] = value

    def residual_edges(p):
        residual_partly(p, 0, 8)
        residual_partly(p, ny - 8, 8)

    def residual_ends():
        for r in range(0, ny, 16):
            residual_partly(0, r, 16)
            residual_partly(nx // 2 - 1, r, 16)

    def residual_mend(p):
        for row, face, halo in ((0, 0, PAD - 1), (ny - 1, ny, PAD + ny)):
            value = rt[p, :, pl.ds(row, 1), :]
            for q in (2 * p, 2 * p + 1):
                value = value + by0[q, :, pl.ds(face, 1), :] * u4[q + 1, :, pl.ds(halo, 1), :]
            rt[p, :, pl.ds(row, 1), :] = value

    def residual_planes():
        for r in range(0, ny, 16):
            own, there = pl.ds(r, 16), pl.ds(r + PAD, 16)
            rt[0, :, own, :] = rt[0, :, own, :] + bx0[0, :, own, :] * u4[0, :, there, :]
            last = nx // 2 - 1
            rt[last, :, own, :] = rt[last, :, own, :] + bx0[nx, :, own, :] * u4[nx + 1, :, there, :]

    loop(1, nx // 2 - 1, 2, residual_inner)
    residual_ends()
    loop(1, nx // 2 - 1, 2, each(residual_edges))
    land(flying)
    residual_planes()
    loop(0, nx // 2, 6, each(residual_mend))

    def put_source(level, p, value):
        _, rows, count = level_dims(dims, level)
        ext, source, first = coarse[level - 1][5:8]
        q = p + reach_of(dims, level)
        own = pl.ds(PAD, rows)
        value = value * 0.125
        if source is not None:
            source[p] = value
        first[q, :, own, :] = ext[q, pl.ds(3 * count, count), own, :] * value

    def first_source(low):
        for first in range(low, low + REACH, 2):
            planes = range(first, first + 2)
            folded = fold_planes([pair_rows(rt, p, ny // 2) for p in planes], table_pair[...])
            for p, value in zip(planes, folded):
                put_source(1, p, value)

    flying = []
    half = nx // 2
    for low_p, ox in ((0, -1), (half - REACH, 1)):
        first_source(low_p)
        flying += send_source(1, ox)
    for low_p in range(REACH, half - REACH, REACH):
        first_source(low_p)
    flying += send_source(1, 0)

    land(wide)
    for level in (1, 2):
        land(flying)
        diag_c, ext, source, c1, c2, c3, c4 = coarse[level - 1][4:11]
        wide_sweeps(dims, level, ext, [c1], (c2, c3, c4))
        planes, rows, count = level_dims(dims, level)
        reach = reach_of(dims, level)
        faces = coarse_faces(ext, count, rows)

        def pair(p, number):
            kept = None
            for q, v, total in neighbour_sums(c4, 0, 0, *faces, 2 * p + reach, 2 * number, PAD, rows):
                value = source[q - reach] - diag_c[q - reach] * v + total
                if kept is None:
                    kept = value
                else:
                    c2[(q - reach) // 2, :, pl.ds(0, rows), :] = kept + value
                    kept = None

        loop(0, planes // 2, 3, pair)
        table = table_pair if level == 1 else small_pair
        folded = fold_planes([pair_rows(c2, p, rows // 2) for p in range(planes // 2)], table[...])
        for p, value in enumerate(folded):
            put_source(level + 1, p, value)
        flying = send_source(level + 1, -1) + send_source(level + 1, 1) + send_source(level + 1, 0)
    land(flying)
    for copy in sent:
        copy.wait_send()


def last_kernel(dims, u4, mid, low, ext3, first3, *refs):
    outs, (c2, c3, c4, top, sem) = refs[:4], refs[4:]
    stores = []
    for level, field in enumerate((u4, mid, low)):
        planes, rows, count = level_dims(dims, level)
        own = pl.ds(reach_of(dims, level) if level else 1, planes)
        for t in range(count):
            copy = pltpu.make_async_copy(
                field.at[own, t, pl.ds(PAD, rows)],
                outs[level].at[:, :, pl.ds(t * LANES, LANES)],
                sem.at[len(stores)],
            )
            copy.start()
            stores.append(copy)
    wide_sweeps(dims, 3, ext3, [first3], (c2, c3, c4))
    planes, rows, _ = level_dims(dims, 3)
    top[...] = c4[pl.ds(reach_of(dims, 3), planes), 0, pl.ds(PAD, rows), pl.ds(0, LANES // 2)]
    copy = pltpu.make_async_copy(top, outs[3], sem.at[len(stores)])
    copy.start()
    for store in stores + [copy]:
        store.wait()


def space(*shape):
    return pltpu.VMEM(shape, F32)


def halo_shape(dims, level):
    x, y, t = level_dims(dims, level)
    around = reach_of(dims, level) if level else 1
    return (x + 2 * around, t, y + 2 * PAD, LANES)


def scratch_of(dims):
    nx, ny, nz = dims
    tiles = nz // LANES
    shapes = [
        space(nx, tiles, ny, LANES),
        space(nx, tiles, ny, LANES),
        space(nx + 1, tiles, ny, LANES),
        space(nx, tiles, ny + 2 * PAD, LANES),
        space(nx, tiles, ny, LANES),
        space(nx, tiles, ny, LANES),
        space(nx, tiles, ny, LANES),
    ]
    shapes += [space(*halo_shape(dims, 0))] * 3
    shapes += [pltpu.VMEM((2 * LANES, LANES), BF16)] * 2
    shapes += [pltpu.VMEM((LANES, LANES), BF16)] * 2
    for level in (1, 2, 3):
        x, y, t = level_dims(dims, level)
        tall = y + 2 * PAD
        shapes += [
            space(x, t, y, LANES),
            space(x + 1, t, y, LANES),
            space(x, t, tall, LANES),
            space(x, t, y, LANES),
            space(x, t, y, LANES),
        ]
        if level < 3:
            whole = halo_shape(dims, level)
            shapes += [space(whole[0], 4 * t, tall, LANES), space(x, t, y, LANES)]
            shapes += [space(*whole)] * 3
    shapes += [
        pltpu.SemaphoreType.DMA((5, 9 + len(CUTS))),
        pltpu.SemaphoreType.DMA((COPIES,)),
        pltpu.SemaphoreType.DMA((COPIES,)),
    ]
    return shapes


def body(counts, *args):
    dims = args[0].shape
    nx, ny, nz = dims
    whole3 = halo_shape(dims, 3)
    kept = [halo_shape(dims, level) for level in range(3)]
    kept += [(whole3[0], 4) + whole3[2:], whole3]
    in_hbm = pl.BlockSpec(memory_space=pltpu.HBM)
    in_vmem = pl.BlockSpec(memory_space=pltpu.VMEM)
    fields = pl.pallas_call(
        functools.partial(kernel, dims, counts),
        out_shape=[pltpu.VMEM(shape, F32) for shape in kept],
        in_specs=[in_hbm] * 5,
        out_specs=[in_vmem] * 5,
        scratch_shapes=scratch_of(dims),
        compiler_params=pltpu.CompilerParams(
            collective_id=0, has_side_effects=True, vmem_limit_bytes=48 * 2**20
        ),
        name="sweep",
    )(*[pltpu.with_memory_space_constraint(x, pltpu.HBM) for x in args])
    return pl.pallas_call(
        functools.partial(last_kernel, dims),
        out_shape=[pltpu.HBM((nx >> k, ny >> k, nz >> k), F32) for k in range(4)],
        in_specs=[in_vmem] * 5,
        out_specs=[in_hbm] * 4,
        scratch_shapes=[space(*whole3)] * 3
        + [space(nx // 8, ny // 8, LANES // 2), pltpu.SemaphoreType.DMA((16,))],
        compiler_params=pltpu.CompilerParams(vmem_limit_bytes=4 * 2**20),
        name="results",
    )(*[pltpu.with_memory_space_constraint(x, pltpu.VMEM) for x in fields])


def solution(mesh):
    spec = P("gx", "gy", None)
    counts = (mesh.shape["gx"], mesh.shape["gy"])
    return jax.shard_map(
        functools.partial(body, counts),
        mesh=mesh,
        in_specs=(spec,) * 5,
        out_specs=(spec,) * 4,
        check_vma=False,
    )
```

```python
import functools

import jax
import jax.numpy as jnp
from jax import lax
from jax.experimental import pallas as pl
from jax.experimental.pallas import tpu as pltpu
from jax.sharding import PartitionSpec as P

DEGREE = 4
CHEB_HIGH = 2.0
CHEB_LOW = 0.25
LANES = 128
PAD = 8
REACH = 4
CUTS = (2, 4, 5)
EARLY = 1
COPIES = 96
MESH = pl.DeviceIdType.MESH
F32 = jnp.float32
BF16 = jnp.bfloat16


def chebyshev_weights():
    theta = 0.5 * (CHEB_HIGH + CHEB_LOW)
    delta = 0.5 * (CHEB_HIGH - CHEB_LOW)
    sigma = theta / delta
    old = 1.0 / sigma
    first, second = [], []
    for _ in range(1, DEGREE):
        new = 1.0 / (2.0 * sigma - old)
        first.append(new * old)
        second.append(2.0 * new / delta)
        old = new
    s1 = 1.0 / theta
    s2 = second[0] * s1
    s3 = second[1] * s2
    s4 = second[2] * s3
    keep = [1.0 + first[k] - second[k] for k in range(3)]
    return (
        (((keep[0] * s1 + second[0]) / s2,), 1.0),
        ((keep[1] * s2 / s3, (second[1] - first[1] * s1) / s3), 1.0),
        ((keep[2] * s3, -first[2] * s2, second[2]), s4),
    )


WEIGHTS = chebyshev_weights()


def loop(low, high, step, fn):
    turns = (high - low) // step

    def turn(i, _):
        fn(low + i * step, step)
        return 0

    if turns == 1:
        fn(low, step)
    elif turns:
        lax.fori_loop(0, turns, turn, 0)
    if low + turns * step < high:
        fn(low + turns * step, high - low - turns * step)


def each(fn):
    def block(first, number):
        for k in range(number):
            fn(first + k)

    return block


def lane_index(shape):
    return lax.broadcasted_iota(jnp.int32, shape, len(shape) - 1)


def z_below(v):
    turned = pltpu.roll(v, 1, 2)
    if v.shape[0] == 1:
        return turned
    before = jnp.concatenate([turned[-1:], turned[:-1]], axis=0)
    return jnp.where(lane_index(v.shape) == 0, before, turned)


def z_above(v):
    turned = pltpu.roll(v, LANES - 1, 2)
    if v.shape[0] == 1:
        return turned
    after = jnp.concatenate([turned[1:], turned[:1]], axis=0)
    return jnp.where(lane_index(v.shape) == LANES - 1, after, turned)


def neighbour_sums(u, du, dr, bx, by, bz, p, number, r, size):
    here = pl.ds(r + dr, size)
    before, v, lower = u[p + du - 1, :, here, :], u[p + du, :, here, :], bx(p, r)
    for k in range(number):
        q = p + k
        after, upper = u[q + du + 1, :, here, :], bx(q + 1, r)
        depth = bz(q, r)
        total = lower * before + upper * after
        total = total + by(q, r) * u[q + du, :, pl.ds(r + dr - 1, size), :]
        total = total + by(q, r + 1) * u[q + du, :, pl.ds(r + dr + 1, size), :]
        yield q, v, total + (depth * z_below(v) + z_above(depth * v))
        before, v, lower = v, after, upper


def inverse_of(diag):
    guess = pl.reciprocal(diag, approx=True)
    return guess * (2.0 - diag * guess)


def fold(values, table):
    high = values.astype(BF16)
    low = (values - high.astype(F32)).astype(BF16)
    both = jnp.dot(jnp.concatenate([high, low], axis=0), table, preferred_element_type=F32)
    return both[: values.shape[0]] + both[values.shape[0] :]


def fold_planes(blocks, table):
    tiles, rows, _ = blocks[0].shape
    if tiles == 1:
        stacked = jnp.concatenate([block[0] for block in blocks], axis=0)
        out = fold(stacked, table)
        return [out[i * rows : (i + 1) * rows][None] for i in range(len(blocks))]
    parts = []
    for block in blocks:
        for t in range(0, tiles, 2):
            parts.append(jnp.concatenate([block[t], block[t + 1]], axis=1))
    out = fold(jnp.concatenate(parts, axis=0), table)
    half = tiles // 2
    result = []
    for i in range(len(blocks)):
        rows_of = [out[(i * half + t) * rows : (i * half + t + 1) * rows] for t in range(half)]
        result.append(jnp.stack(rows_of, axis=0))
    return result


def level_dims(dims, level):
    nx, ny, nz = dims
    return nx >> level, ny >> level, max((nz // LANES) >> level, 1)


def reach_of(dims, level):
    return min(REACH, dims[0] >> level)


def combine(weights, v, total, inverse, older):
    factors, scale = weights
    change = inverse * total
    if scale != 1.0:
        change = change * scale
    value = factors[0] * v
    for factor, field in zip(factors[1:], older):
        value = value + factor * field
    return value + change


def wide_sweep(dims, level, ext, k, fields, low, high, windows, step):
    count = level_dims(dims, level)[2]
    u, older, target = fields[k], fields[:k][::-1], fields[k + 1]

    def sweep(p, number):
        for first, size in windows:
            place = pl.ds(first, size)
            for q, v, total in neighbour_sums(u, 0, 0, *coarse_faces(ext, count, size), p, number, first, size):
                past = [field[q, :, place, :] for field in older]
                inverse = ext[q, pl.ds(3 * count, count), place, :]
                target[q, :, place, :] = combine(WEIGHTS[k], v, total, inverse, past)

    loop(low, high, step, sweep)


def wide_sweeps(dims, level, ext, fields):
    planes, rows, _ = level_dims(dims, level)
    whole = planes + 2 * reach_of(dims, level)
    for k in range(3):
        window = (PAD - REACH, rows + 2 * REACH)
        if k == 2 and level == 3:
            window = (PAD, rows)
        wide_sweep(dims, level, ext, k, fields, k + 1, whole - k - 1, [window], whole)


def coarse_faces(ext, count, length):
    def face(a):
        return lambda p, r: ext[p, pl.ds(a * count, count), pl.ds(r, length), :]

    return face(0), face(1), face(2)


def kernel(dims, counts, *refs):
    nx, ny, nz = dims
    tiles = nz // LANES
    refs = list(refs)
    rhs_h, alpha_h, bx_h, by_h, bz_h = refs[:5]
    u4, mid, low, ext3, first3 = refs[5:10]
    f0, al0, bx0, by0, bz0, inv0, diag0, u1, u2, u3 = refs[10:20]
    rt = al0
    table_pair, table_even, small_pair, small_even = refs[20:24]
    coarse = [refs[24:34] + [mid], refs[34:44] + [low], refs[44:49] + [ext3, None, first3]]
    in_sem, send_sem, recv_sem = refs[49:52]

    gx, gy = lax.axis_index("gx"), lax.axis_index("gy")
    cx, cy = counts

    def device(ox, oy):
        return (lax.rem(gx + ox + cx, cx), lax.rem(gy + oy + cy, cy))

    around = [(ox, oy) for ox in (-1, 0, 1) for oy in (-1, 0, 1) if (ox, oy) != (0, 0)]

    used = [0]
    sent = []

    def send(src, dst, where):
        index = used[0]
        used[0] += 1
        copy = pltpu.make_async_remote_copy(
            src_ref=src,
            dst_ref=dst,
            send_sem=send_sem.at[index],
            recv_sem=recv_sem.at[index],
            device_id=device(*where),
            device_id_type=MESH,
        )
        copy.start()
        sent.append(copy)
        return copy

    locals_of = ((bx_h, bx0), (by_h, by0), (bz_h, bz0), (alpha_h, al0), (rhs_h, f0))
    edge = 8
    cuts = [2] + [nx * k // 6 for k in CUTS] + [nx - 2]

    def pieces(a):
        more_rows, more_planes = (edge if a == 1 else 0), (1 if a == 0 else 0)
        low, low2, top, top2 = edge + more_rows, 2 * edge + more_rows, ny - edge, ny - 2 * edge
        one, two = 1 + more_planes, 2 + more_planes
        parts = [((0, nx), (0, low)), ((0, nx), (top, ny)), ((0, one), (low, top)), ((nx - 1, nx), (low, top))]
        parts += [((one, nx - 1), (low, low2)), ((one, nx - 1), (top2, top))]
        parts += [((one, two), (low2, top2)), ((nx - 2, nx - 1), (low2, top2))]
        for g in range(len(cuts) - 1):
            parts.append(((max(cuts[g], two), cuts[g + 1]), (low2, top2)))
        return parts

    def part_of(ref, planes, rows):
        return ref.at[pl.ds(planes[0], planes[1] - planes[0]), :, pl.ds(rows[0], rows[1] - rows[0])]

    def load(n):
        for a, (src, dst) in enumerate(locals_of):
            planes, rows = pieces(a)[n]
            for t in range(tiles):
                pltpu.make_async_copy(
                    part_of(src, planes, (t * LANES, (t + 1) * LANES)).at[:, pl.ds(rows[0], rows[1] - rows[0])],
                    part_of(dst, planes, rows).at[:, t],
                    in_sem.at[a, n],
                ).start()

    def wait_input(n):
        for a, (_, dst) in enumerate(locals_of):
            part = part_of(dst, *pieces(a)[n])
            pltpu.make_async_copy(part, part, in_sem.at[a, n]).wait()

    barrier = pltpu.get_barrier_semaphore()
    for where in around:
        pl.semaphore_signal(barrier, inc=1, device_id=device(*where), device_id_type=MESH)
    for n in range(4):
        load(n)

    def fill(ref, even):
        k = lax.broadcasted_iota(jnp.int32, ref.shape, 0)
        c = lax.broadcasted_iota(jnp.int32, ref.shape, 1)
        if ref.shape[0] == LANES:
            c = c % (LANES // 2)
        hit = k == 2 * c if even else k // 2 == c
        ref[...] = jnp.where(hit, 1.0, 0.0).astype(BF16)

    pl.semaphore_wait(barrier, len(around))

    halo = []
    for t in range(tiles):
        lanes = pl.ds(t * LANES, LANES)
        halo.append(send(by_h.at[:, pl.ds(0, 1), lanes], by0.at[:, t, pl.ds(ny, 1)], (0, -1)))
    for t in range(tiles):
        lanes = pl.ds(t * LANES, LANES)
        halo.append(send(bx_h.at[0, :, lanes], bx0.at[nx, t], (-1, 0)))

    for n in range(4, 7 + len(cuts)):
        load(n)

    fill(table_pair, False)
    fill(table_even, True)
    fill(small_pair, False)
    fill(small_even, True)

    def start_rows(p, r, size):
        rows = pl.ds(r, size)
        depth = bz0[p, :, rows, :]
        diag = al0[p, :, rows, :] + bx0[p, :, rows, :] + bx0[p + 1, :, rows, :]
        diag = diag + by0[p, :, rows, :] + by0[p, :, pl.ds(r + 1, size), :]
        diag = diag + depth + z_above(depth)
        inverse = inverse_of(diag)
        diag0[p, :, rows, :] = diag
        inv0[p, :, rows, :] = inverse
        u1[p + 1, :, pl.ds(r + PAD, size), :] = inverse * f0[p, :, rows, :]

    def start_ends(j):
        r = pl.multiple_of(j * 16, 16)
        start_rows(0, r, 16)
        start_rows(nx - 1, r, 16)

    def start_edges(p):
        start_rows(p, 0, 8)
        start_rows(p, ny - 8, 8)

    def start_next(p):
        start_rows(p, edge, edge)
        start_rows(p, ny - 2 * edge, edge)

    def start_inner(p):
        for r in range(2 * edge, ny - 2 * edge, 16):
            start_rows(p, r, 16)

    def send_planes(u):
        rows = pl.ds(PAD, ny)
        return [
            send(u.at[1, :, rows], u.at[nx + 1, :, rows], (-1, 0)),
            send(u.at[nx, :, rows], u.at[0, :, rows], (1, 0)),
        ]

    def send_rows(u):
        planes = pl.ds(1, nx)
        return [
            send(u.at[planes, :, pl.ds(PAD, 1)], u.at[planes, :, pl.ds(PAD + ny, 1)], (0, -1)),
            send(u.at[planes, :, pl.ds(PAD + ny - 1, 1)], u.at[planes, :, pl.ds(PAD - 1, 1)], (0, 1)),
        ]

    def land(copies):
        for copy in copies:
            copy.wait_recv()

    def pair_rows(ref, p, size):
        return ref[p, :, pl.ds(0, size, 2), :] + ref[p, :, pl.ds(1, size, 2), :]

    def restrict_block(level, source, table_p, table_e, plane_list, with_x):
        al, bx, by, bz = source
        al_c, bx_c, by_c, bz_c = coarse[level - 1][:4]
        rows = ny >> level
        more = rows + PAD
        planes = plane_list
        folded = fold_planes([pair_rows(bx, 2 * p, rows) for p in planes], table_p)
        for p, value in zip(planes, folded):
            bx_c[p, :, pl.ds(0, rows), :] = value * 0.0625
        if not with_x:
            return
        folded = fold_planes(
            [by[2 * p, :, pl.ds(0, more, 2), :] + by[2 * p + 1, :, pl.ds(0, more, 2), :] for p in planes], table_p
        )
        for p, value in zip(planes, folded):
            by_c[p, :, pl.ds(0, more), :] = value * 0.0625
        folded = fold_planes([pair_rows(bz, 2 * p, rows) + pair_rows(bz, 2 * p + 1, rows) for p in planes], table_e)
        for p, value in zip(planes, folded):
            bz_c[p, :, pl.ds(0, rows), :] = value * 0.0625
        folded = fold_planes([pair_rows(al, 2 * p, rows) + pair_rows(al, 2 * p + 1, rows) for p in planes], table_p)
        for p, value in zip(planes, folded):
            al_c[p, :, pl.ds(0, rows), :] = value * 0.125

    def coarse_plane(level, p):
        al, bx, by, bz, diag_c, ext = coarse[level - 1][:6]
        _, rows, count = level_dims(dims, level)
        reach = reach_of(dims, level)
        own = pl.ds(0, rows)
        lower_x, lower_y, depth = bx[p, :, own, :], by[p, :, own, :], bz[p, :, own, :]
        diag = al[p, :, own, :] + lower_x + bx[p + 1, :, own, :]
        diag = diag + lower_y + by[p, :, pl.ds(1, rows), :] + depth + z_above(depth)
        diag_c[p, :, :, :] = diag
        place = pl.ds(PAD, rows)
        for a, value in enumerate((lower_x, lower_y, depth, inverse_of(diag))):
            ext[p + reach, pl.ds(a * count, count), place, :] = value

    def send_outer(field, level, ox, oy, part, below=REACH, above=REACH):
        planes, rows, _ = level_dims(dims, level)
        reach = reach_of(dims, level)
        depth = {-1: min(below, reach), 0: planes, 1: min(above, reach)}[ox]
        width = {-1: below, 0: rows, 1: above}[oy]
        from_x = {-1: reach, 0: reach, 1: reach + planes - depth}[ox]
        to_x = {-1: reach + planes, 0: reach, 1: reach - depth}[ox]
        from_y = {-1: PAD, 0: PAD, 1: PAD + rows - width}[oy]
        to_y = {-1: PAD + rows, 0: PAD, 1: PAD - width}[oy]
        return send(
            field.at[pl.ds(from_x, depth), part, pl.ds(from_y, width)],
            field.at[pl.ds(to_x, depth), part, pl.ds(to_y, width)],
            (ox, oy),
        )

    sides = [where for where in around if 0 in where]
    corners = [where for where in around if 0 not in where]

    def send_wide(level, places, arrays, below=REACH, above=REACH - 1):
        count = level_dims(dims, level)[2]
        part = pl.ds(arrays[0] * count, (arrays[1] - arrays[0]) * count)
        return [send_outer(coarse[level - 1][5], level, ox, oy, part, below, above) for ox, oy in places]

    def send_source(level, ox):
        part = pl.ds(0, level_dims(dims, level)[2])
        field = coarse[level - 1][7]
        return [send_outer(field, level, ox, oy, part) for oy in (-1, 1, 0) if (ox, oy) != (0, 0)]

    fine_coeffs = (al0, bx0, by0, bz0)

    def first_coarse(p):
        restrict_block(1, fine_coeffs, table_pair[...], table_even[...], [2 * p, 2 * p + 1], True)

    def first_plane(p):
        coarse_plane(1, p)

    def lower_coarse():
        for level in (2, 3):
            tables = (table_pair, table_even) if level == 2 else (small_pair, small_even)
            planes = nx >> level
            source = coarse[level - 2][:4]
            restrict_block(level, source, tables[0][...], tables[1][...], list(range(planes)), True)
            restrict_block(level, source, tables[0][...], tables[1][...], [planes], False)
            for p in range(planes):
                coarse_plane(level, p)

    def fine_face(ref, size):
        return lambda p, r: ref[p, :, pl.ds(r, size), :]

    def fine_sums(u, p, number, r, size):
        faces = fine_face(bx0, size), fine_face(by0, size), fine_face(bz0, size)
        return neighbour_sums(u, 1, PAD, *faces, p, number, r, size)

    def partial_sum(u, q, r, size):
        rows, here = pl.ds(r, size), pl.ds(r + PAD, size)
        v, depth = u[q + 1, :, here, :], bz0[q, :, rows, :]
        total = depth * z_below(v) + z_above(depth * v)
        ends = isinstance(q, int)
        if not (ends and q == 0):
            total = total + bx0[q, :, rows, :] * u[q, :, here, :]
        if not (ends and q == nx - 1):
            total = total + bx0[q + 1, :, rows, :] * u[q + 2, :, here, :]
        row = lax.broadcasted_iota(jnp.int32, v.shape, 1)
        if r == 0:
            below = jnp.where(row == 0, 0.0, pltpu.roll(v, 1, 1))
        else:
            below = u[q + 1, :, pl.ds(r + PAD - 1, size), :]
        if r + size == ny:
            above = jnp.where(row == size - 1, 0.0, pltpu.roll(v, size - 1, 1))
        else:
            above = u[q + 1, :, pl.ds(r + PAD + 1, size), :]
        return v, total + by0[q, :, rows, :] * below + by0[q, :, pl.ds(r + 1, size), :] * above

    def fine_sweep(weights, fields, target):
        u, older = fields[0], fields[1:]

        def update(p, number, r, size):
            place = pl.ds(r + PAD, size)
            for q, v, total in fine_sums(u, p, number, r, size):
                past = [field[q + 1, :, place, :] for field in older]
                inverse = inv0[q, :, pl.ds(r, size), :]
                target[q + 1, :, place, :] = combine(weights, v, total, inverse, past)

        def partly(q, r, size):
            v, total = partial_sum(u, q, r, size)
            rows, here = pl.ds(r, size), pl.ds(r + PAD, size)
            past = [field[q + 1, :, here, :] for field in older]
            target[q + 1, :, here, :] = combine(weights, v, total, inv0[q, :, rows, :], past)

        def mend(q, rows, face, halo):
            change = inv0[q, :, rows, :] * face * halo
            if weights[1] != 1.0:
                change = change * weights[1]
            here = pl.ds(rows.start + PAD, rows.size)
            target[q + 1, :, here, :] = target[q + 1, :, here, :] + change

        def mend_rows(q):
            for row, face, halo in ((0, 0, PAD - 1), (ny - 1, ny, PAD + ny)):
                mend(q, pl.ds(row, 1), by0[q, :, pl.ds(face, 1), :], u[q + 1, :, pl.ds(halo, 1), :])

        def end_rows(q):
            partly(q, 0, 8)
            partly(q, ny - 8, 8)

        def inner(p, number):
            for r in range(8, ny - 8, 8):
                update(p, number, r, 8)

        def before():
            for r in range(0, ny, 16):
                partly(0, r, 16)
                partly(nx - 1, r, 16)
            loop(1, nx - 1, 4, each(end_rows))

        def outer():
            for r in range(0, ny, 16):
                rows, here = pl.ds(r, 16), pl.ds(r + PAD, 16)
                mend(0, rows, bx0[0, :, rows, :], u[0, :, here, :])
                mend(nx - 1, rows, bx0[nx, :, rows, :], u[nx + 1, :, here, :])
            mend_rows(0)
            mend_rows(nx - 1)
            copies = send_planes(target)
            loop(1, nx - 1, 11, each(mend_rows))
            return copies + send_rows(target)

        def deep(p, number):
            for r in range(16, ny - 16, 8):
                update(p, number, r, 8)

        def shell(p, number):
            update(p, number, 8, 8)
            update(p, number, ny - 16, 8)

        def rest():
            loop(1, nx - 1, 4, shell)
            deep(1, 1)
            deep(nx - 2, 1)

        return before, outer, inner, lambda: loop(2, nx - 2, 4, deep), rest


    sweeps = [fine_sweep(WEIGHTS[k], (u3, u2, u1)[2 - k :], (u2, u3, u4)[k]) for k in range(3)]

    for n in range(4):
        wait_input(n)
    land(halo)
    loop(0, ny // 16, 2, each(start_ends))
    flying = send_planes(u1)
    loop(1, nx - 1, 4, each(start_edges))
    flying += send_rows(u1)
    restrict_block(1, fine_coeffs, table_pair[...], table_even[...], [nx // 2], False)
    for n in range(4, 8):
        wait_input(n)
    loop(1, nx - 1, 4, each(start_next))
    start_inner(1)
    start_inner(nx - 2)
    done = 0
    for g in range(len(cuts) - 1):
        wait_input(8 + g)
        final = g == len(cuts) - 2
        loop(max(cuts[g] - 1, 2), nx - 2 if final else cuts[g + 1] - 1, 2, each(start_inner))
        if g == EARLY - 1:
            sweeps[0][0]()
        if g == EARLY:
            land(flying)
            flying = sweeps[0][1]()
        ready = nx // 4 if final else cuts[g + 1] // 4
        loop(done, ready, 1, each(first_coarse))
        done = ready
    loop(0, nx // 2, 4, each(first_plane))
    wide = send_wide(1, sides, (0, 2))
    loop(1, nx - 1, 4, sweeps[0][2])
    for k in (1, 2):
        sweeps[k][0]()
        land(flying)
        flying = sweeps[k][1]()
        if k == 1:
            wide += send_wide(1, sides, (2, 4), REACH - 1) + send_wide(1, corners, (0, 4))
        else:
            wide += send_wide(2, around, (0, 4)) + send_wide(3, around, (0, 4))
        if k == 1:
            loop(1, nx - 1, 4, sweeps[1][2])
            lower_coarse()
            sweeps[2][3]()
        else:
            sweeps[2][4]()

    def residual_rows(p, number, rows):
        for r in rows:
            own = pl.ds(r, 8)
            kept = None
            for q, v, total in fine_sums(u4, 2 * p, 2 * number, r, 8):
                value = f0[q, :, own, :] - diag0[q, :, own, :] * v + total
                if kept is None:
                    kept = q, value
                else:
                    rt[kept[0] // 2, :, own, :] = kept[1] + value
                    kept = None

    def residual_inner(p, number):
        residual_rows(p, number, range(8, ny - 8, 8))

    def residual_partly(p, r, size):
        own = pl.ds(r, size)
        value = 0.0
        for q in (2 * p, 2 * p + 1):
            v, total = partial_sum(u4, q, r, size)
            value = value + (f0[q, :, own, :] - diag0[q, :, own, :] * v + total)
        rt[p, :, own, :] = value

    def residual_edges(p):
        residual_partly(p, 0, 8)
        residual_partly(p, ny - 8, 8)

    def residual_ends():
        for r in range(0, ny, 16):
            residual_partly(0, r, 16)
            residual_partly(nx // 2 - 1, r, 16)

    def residual_mend(p):
        for row, face, halo in ((0, 0, PAD - 1), (ny - 1, ny, PAD + ny)):
            value = rt[p, :, pl.ds(row, 1), :]
            for q in (2 * p, 2 * p + 1):
                value = value + by0[q, :, pl.ds(face, 1), :] * u4[q + 1, :, pl.ds(halo, 1), :]
            rt[p, :, pl.ds(row, 1), :] = value

    def residual_planes():
        for r in range(0, ny, 16):
            own, there = pl.ds(r, 16), pl.ds(r + PAD, 16)
            rt[0, :, own, :] = rt[0, :, own, :] + bx0[0, :, own, :] * u4[0, :, there, :]
            last = nx // 2 - 1
            rt[last, :, own, :] = rt[last, :, own, :] + bx0[nx, :, own, :] * u4[nx + 1, :, there, :]

    loop(1, nx // 2 - 1, 2, residual_inner)
    residual_ends()
    loop(1, nx // 2 - 1, 2, each(residual_edges))
    land(flying)
    residual_planes()
    loop(0, nx // 2, 6, each(residual_mend))

    def put_source(level, p, value):
        _, rows, count = level_dims(dims, level)
        ext, source, first = coarse[level - 1][5:8]
        q = p + reach_of(dims, level)
        own = pl.ds(PAD, rows)
        value = value * 0.125
        if source is not None:
            source[p] = value
        first[q, :, own, :] = ext[q, pl.ds(3 * count, count), own, :] * value

    def first_source(low):
        for first in range(low, low + REACH, 2):
            planes = range(first, first + 2)
            folded = fold_planes([pair_rows(rt, p, ny // 2) for p in planes], table_pair[...])
            for p, value in zip(planes, folded):
                put_source(1, p, value)

    flying = []
    half = nx // 2
    for low_p, ox in ((0, -1), (half - REACH, 1)):
        first_source(low_p)
        flying += send_source(1, ox)
    for low_p in range(REACH, half - REACH, REACH):
        first_source(low_p)
    flying += send_source(1, 0)

    land(wide)
    for level in (1, 2):
        diag_c, ext, source, c1, c2, c3, c4 = coarse[level - 1][4:11]
        fields = [c1, c2, c3, c4]
        planes, rows, count = level_dims(dims, level)
        reach = reach_of(dims, level)
        if level == 1:
            middle = [(reach + 1 + k, reach + planes - 1 - k) for k in range(3)]
            for k, (low_p, high_p) in enumerate(middle):
                first, last = PAD + REACH + k, PAD + rows - REACH - k
                starts = list(range(first, last - 8, 8)) + [last - 8]
                wide_sweep(dims, 1, ext, k, fields, low_p, high_p, [(r, 8) for r in starts], 5)
            land(flying)
            for k, (low_p, high_p) in enumerate(middle):
                full = [(PAD - REACH, 24), (PAD - REACH + 24, rows + 2 * REACH - 24)]
                edges = [(PAD - REACH + k, 8), (PAD + rows - REACH - k, 8)]
                wide_sweep(dims, 1, ext, k, fields, k + 1, low_p, full, 4)
                wide_sweep(dims, 1, ext, k, fields, high_p, planes + 2 * reach - k - 1, full, 4)
                wide_sweep(dims, 1, ext, k, fields, low_p, high_p, edges, 5)
        else:
            land(flying)
            wide_sweeps(dims, level, ext, fields)
        faces = coarse_faces(ext, count, rows)

        def pair(p, number):
            kept = None
            for q, v, total in neighbour_sums(c4, 0, 0, *faces, 2 * p + reach, 2 * number, PAD, rows):
                value = source[q - reach] - diag_c[q - reach] * v + total
                if kept is None:
                    kept = value
                else:
                    c2[(q - reach) // 2, :, pl.ds(0, rows), :] = kept + value
                    kept = None

        loop(0, planes // 2, 3, pair)
        table = table_pair if level == 1 else small_pair
        folded = fold_planes([pair_rows(c2, p, rows // 2) for p in range(planes // 2)], table[...])
        for p, value in enumerate(folded):
            put_source(level + 1, p, value)
        flying = send_source(level + 1, -1) + send_source(level + 1, 1) + send_source(level + 1, 0)
    land(flying)
    for copy in sent:
        copy.wait_send()


def last_kernel(dims, u4, mid, low, ext3, first3, *refs):
    outs, (c2, c3, c4, top, sem) = refs[:4], refs[4:]
    stores = []
    for level, field in enumerate((u4, mid, low)):
        planes, rows, count = level_dims(dims, level)
        own = pl.ds(reach_of(dims, level) if level else 1, planes)
        for t in range(count):
            copy = pltpu.make_async_copy(
                field.at[own, t, pl.ds(PAD, rows)],
                outs[level].at[:, :, pl.ds(t * LANES, LANES)],
                sem.at[len(stores)],
            )
            copy.start()
            stores.append(copy)
    wide_sweeps(dims, 3, ext3, [first3, c2, c3, c4])
    planes, rows, _ = level_dims(dims, 3)
    top[...] = c4[pl.ds(reach_of(dims, 3), planes), 0, pl.ds(PAD, rows), pl.ds(0, LANES // 2)]
    copy = pltpu.make_async_copy(top, outs[3], sem.at[len(stores)])
    copy.start()
    for store in stores + [copy]:
        store.wait()


def space(*shape):
    return pltpu.VMEM(shape, F32)


def halo_shape(dims, level):
    x, y, t = level_dims(dims, level)
    around = reach_of(dims, level) if level else 1
    return (x + 2 * around, t, y + 2 * PAD, LANES)


def scratch_of(dims):
    nx, ny, nz = dims
    tiles = nz // LANES
    shapes = [
        space(nx, tiles, ny, LANES),
        space(nx, tiles, ny, LANES),
        space(nx + 1, tiles, ny, LANES),
        space(nx, tiles, ny + 2 * PAD, LANES),
        space(nx, tiles, ny, LANES),
        space(nx, tiles, ny, LANES),
        space(nx, tiles, ny, LANES),
    ]
    shapes += [space(*halo_shape(dims, 0))] * 3
    shapes += [pltpu.VMEM((2 * LANES, LANES), BF16)] * 2
    shapes += [pltpu.VMEM((LANES, LANES), BF16)] * 2
    for level in (1, 2, 3):
        x, y, t = level_dims(dims, level)
        tall = y + 2 * PAD
        shapes += [
            space(x, t, y, LANES),
            space(x + 1, t, y, LANES),
            space(x, t, tall, LANES),
            space(x, t, y, LANES),
            space(x, t, y, LANES),
        ]
        if level < 3:
            whole = halo_shape(dims, level)
            shapes += [space(whole[0], 4 * t, tall, LANES), space(x, t, y, LANES)]
            shapes += [space(*whole)] * 3
    shapes += [
        pltpu.SemaphoreType.DMA((5, 9 + len(CUTS))),
        pltpu.SemaphoreType.DMA((COPIES,)),
        pltpu.SemaphoreType.DMA((COPIES,)),
    ]
    return shapes


def body(counts, *args):
    dims = args[0].shape
    nx, ny, nz = dims
    whole3 = halo_shape(dims, 3)
    kept = [halo_shape(dims, level) for level in range(3)]
    kept += [(whole3[0], 4) + whole3[2:], whole3]
    in_hbm = pl.BlockSpec(memory_space=pltpu.HBM)
    in_vmem = pl.BlockSpec(memory_space=pltpu.VMEM)
    fields = pl.pallas_call(
        functools.partial(kernel, dims, counts),
        out_shape=[pltpu.VMEM(shape, F32) for shape in kept],
        in_specs=[in_hbm] * 5,
        out_specs=[in_vmem] * 5,
        scratch_shapes=scratch_of(dims),
        compiler_params=pltpu.CompilerParams(
            collective_id=0, has_side_effects=True, vmem_limit_bytes=48 * 2**20
        ),
        name="sweep",
    )(*[pltpu.with_memory_space_constraint(x, pltpu.HBM) for x in args])
    return pl.pallas_call(
        functools.partial(last_kernel, dims),
        out_shape=[pltpu.HBM((nx >> k, ny >> k, nz >> k), F32) for k in range(4)],
        in_specs=[in_vmem] * 5,
        out_specs=[in_hbm] * 4,
        scratch_shapes=[space(*whole3)] * 3
        + [space(nx // 8, ny // 8, LANES // 2), pltpu.SemaphoreType.DMA((16,))],
        compiler_params=pltpu.CompilerParams(vmem_limit_bytes=4 * 2**20),
        name="results",
    )(*[pltpu.with_memory_space_constraint(x, pltpu.VMEM) for x in fields])


def solution(mesh):
    spec = P("gx", "gy", None)
    counts = (mesh.shape["gx"], mesh.shape["gy"])
    return jax.shard_map(
        functools.partial(body, counts),
        mesh=mesh,
        in_specs=(spec,) * 5,
        out_specs=(spec,) * 4,
        check_vma=False,
    )
```

```python
import functools

import jax
import jax.numpy as jnp
from jax import lax
from jax.experimental import pallas as pl
from jax.experimental.pallas import tpu as pltpu
from jax.sharding import PartitionSpec as P

DEGREE = 4
CHEB_HIGH = 2.0
CHEB_LOW = 0.25
LANES = 128
PAD = 8
REACH = 4
CUTS = (2, 4, 5)
EARLY = 1
COPIES = 96
MESH = pl.DeviceIdType.MESH
F32 = jnp.float32
BF16 = jnp.bfloat16


def chebyshev_weights():
    theta = 0.5 * (CHEB_HIGH + CHEB_LOW)
    delta = 0.5 * (CHEB_HIGH - CHEB_LOW)
    sigma = theta / delta
    old = 1.0 / sigma
    first, second = [], []
    for _ in range(1, DEGREE):
        new = 1.0 / (2.0 * sigma - old)
        first.append(new * old)
        second.append(2.0 * new / delta)
        old = new
    s1 = 1.0 / theta
    s2 = second[0] * s1
    s3 = second[1] * s2
    s4 = second[2] * s3
    keep = [1.0 + first[k] - second[k] for k in range(3)]
    return (
        (((keep[0] * s1 + second[0]) / s2,), 1.0),
        ((keep[1] * s2 / s3, (second[1] - first[1] * s1) / s3), 1.0),
        ((keep[2] * s3, -first[2] * s2, second[2]), s4),
    )


WEIGHTS = chebyshev_weights()


def loop(low, high, step, fn):
    turns = (high - low) // step

    def turn(i, _):
        fn(low + i * step, step)
        return 0

    if turns == 1:
        fn(low, step)
    elif turns:
        lax.fori_loop(0, turns, turn, 0)
    if low + turns * step < high:
        fn(low + turns * step, high - low - turns * step)


def each(fn):
    def block(first, number):
        for k in range(number):
            fn(first + k)

    return block


def lane_index(shape):
    return lax.broadcasted_iota(jnp.int32, shape, len(shape) - 1)


def z_below(v):
    turned = pltpu.roll(v, 1, 2)
    if v.shape[0] == 1:
        return turned
    before = jnp.concatenate([turned[-1:], turned[:-1]], axis=0)
    return jnp.where(lane_index(v.shape) == 0, before, turned)


def z_above(v):
    turned = pltpu.roll(v, LANES - 1, 2)
    if v.shape[0] == 1:
        return turned
    after = jnp.concatenate([turned[1:], turned[:1]], axis=0)
    return jnp.where(lane_index(v.shape) == LANES - 1, after, turned)


def neighbour_sums(u, du, dr, bx, by, bz, p, number, r, size):
    here = pl.ds(r + dr, size)
    before, v, lower = u[p + du - 1, :, here, :], u[p + du, :, here, :], bx(p, r)
    for k in range(number):
        q = p + k
        after, upper = u[q + du + 1, :, here, :], bx(q + 1, r)
        depth = bz(q, r)
        total = lower * before + upper * after
        total = total + by(q, r) * u[q + du, :, pl.ds(r + dr - 1, size), :]
        total = total + by(q, r + 1) * u[q + du, :, pl.ds(r + dr + 1, size), :]
        yield q, v, total + (depth * z_below(v) + z_above(depth * v))
        before, v, lower = v, after, upper


def inverse_of(diag):
    guess = pl.reciprocal(diag, approx=True)
    return guess * (2.0 - diag * guess)


def fold(values, table):
    high = values.astype(BF16)
    low = (values - high.astype(F32)).astype(BF16)
    both = jnp.dot(jnp.concatenate([high, low], axis=0), table, preferred_element_type=F32)
    return both[: values.shape[0]] + both[values.shape[0] :]


def fold_planes(blocks, table):
    tiles, rows, _ = blocks[0].shape
    if tiles == 1:
        stacked = jnp.concatenate([block[0] for block in blocks], axis=0)
        out = fold(stacked, table)
        return [out[i * rows : (i + 1) * rows][None] for i in range(len(blocks))]
    parts = []
    for block in blocks:
        for t in range(0, tiles, 2):
            parts.append(jnp.concatenate([block[t], block[t + 1]], axis=1))
    out = fold(jnp.concatenate(parts, axis=0), table)
    half = tiles // 2
    result = []
    for i in range(len(blocks)):
        rows_of = [out[(i * half + t) * rows : (i * half + t + 1) * rows] for t in range(half)]
        result.append(jnp.stack(rows_of, axis=0))
    return result


def level_dims(dims, level):
    nx, ny, nz = dims
    return nx >> level, ny >> level, max((nz // LANES) >> level, 1)


def reach_of(dims, level):
    return min(REACH, dims[0] >> level)


def combine(weights, v, total, inverse, older):
    factors, scale = weights
    change = inverse * total
    if scale != 1.0:
        change = change * scale
    value = factors[0] * v
    for factor, field in zip(factors[1:], older):
        value = value + factor * field
    return value + change


def wide_sweep(dims, level, ext, k, fields, low, high, windows, step):
    count = level_dims(dims, level)[2]
    u, older, target = fields[k], fields[:k][::-1], fields[k + 1]

    def sweep(p, number):
        for first, size in windows:
            place = pl.ds(first, size)
            for q, v, total in neighbour_sums(u, 0, 0, *coarse_faces(ext, count, size), p, number, first, size):
                past = [field[q, :, place, :] for field in older]
                inverse = ext[q, pl.ds(3 * count, count), place, :]
                target[q, :, place, :] = combine(WEIGHTS[k], v, total, inverse, past)

    loop(low, high, step, sweep)


def wide_sweeps(dims, level, ext, fields):
    planes, rows, _ = level_dims(dims, level)
    whole = planes + 2 * reach_of(dims, level)
    for k in range(3):
        window = (PAD - REACH, rows + 2 * REACH)
        if k == 2 and level == 3:
            window = (PAD, rows)
        wide_sweep(dims, level, ext, k, fields, k + 1, whole - k - 1, [window], whole)


def coarse_faces(ext, count, length):
    def face(a):
        return lambda p, r: ext[p, pl.ds(a * count, count), pl.ds(r, length), :]

    return face(0), face(1), face(2)


def kernel(dims, counts, *refs):
    nx, ny, nz = dims
    tiles = nz // LANES
    refs = list(refs)
    rhs_h, alpha_h, bx_h, by_h, bz_h = refs[:5]
    u4, mid, low, ext3, first3 = refs[5:10]
    f0, al0, bx0, by0, bz0, inv0, diag0, u1, u2, u3 = refs[10:20]
    rt = al0
    table_pair, table_even, small_pair, small_even = refs[20:24]
    coarse = [refs[24:34] + [mid], refs[34:44] + [low], refs[44:49] + [ext3, None, first3]]
    in_sem, send_sem, recv_sem = refs[49:52]

    gx, gy = lax.axis_index("gx"), lax.axis_index("gy")
    cx, cy = counts

    def device(ox, oy):
        return (lax.rem(gx + ox + cx, cx), lax.rem(gy + oy + cy, cy))

    around = [(ox, oy) for ox in (-1, 0, 1) for oy in (-1, 0, 1) if (ox, oy) != (0, 0)]

    used = [0]
    sent = []

    def send(src, dst, where):
        index = used[0]
        used[0] += 1
        copy = pltpu.make_async_remote_copy(
            src_ref=src,
            dst_ref=dst,
            send_sem=send_sem.at[index],
            recv_sem=recv_sem.at[index],
            device_id=device(*where),
            device_id_type=MESH,
        )
        copy.start()
        sent.append(copy)
        return copy

    locals_of = ((bx_h, bx0), (by_h, by0), (bz_h, bz0), (alpha_h, al0), (rhs_h, f0))
    edge = 8
    cuts = [2] + [nx * k // 6 for k in CUTS] + [nx - 2]

    def pieces(a):
        more_rows, more_planes = (edge if a == 1 else 0), (1 if a == 0 else 0)
        low, low2, top, top2 = edge + more_rows, 2 * edge + more_rows, ny - edge, ny - 2 * edge
        one, two = 1 + more_planes, 2 + more_planes
        parts = [((0, nx), (0, low)), ((0, nx), (top, ny)), ((0, one), (low, top)), ((nx - 1, nx), (low, top))]
        parts += [((one, nx - 1), (low, low2)), ((one, nx - 1), (top2, top))]
        parts += [((one, two), (low2, top2)), ((nx - 2, nx - 1), (low2, top2))]
        for g in range(len(cuts) - 1):
            parts.append(((max(cuts[g], two), cuts[g + 1]), (low2, top2)))
        return parts

    def part_of(ref, planes, rows):
        return ref.at[pl.ds(planes[0], planes[1] - planes[0]), :, pl.ds(rows[0], rows[1] - rows[0])]

    def load(n):
        for a, (src, dst) in enumerate(locals_of):
            planes, rows = pieces(a)[n]
            for t in range(tiles):
                pltpu.make_async_copy(
                    part_of(src, planes, (t * LANES, (t + 1) * LANES)).at[:, pl.ds(rows[0], rows[1] - rows[0])],
                    part_of(dst, planes, rows).at[:, t],
                    in_sem.at[a, n],
                ).start()

    def wait_input(n):
        for a, (_, dst) in enumerate(locals_of):
            part = part_of(dst, *pieces(a)[n])
            pltpu.make_async_copy(part, part, in_sem.at[a, n]).wait()

    barrier = pltpu.get_barrier_semaphore()
    for where in around:
        pl.semaphore_signal(barrier, inc=1, device_id=device(*where), device_id_type=MESH)
    for n in range(4):
        load(n)

    def fill(ref, even):
        k = lax.broadcasted_iota(jnp.int32, ref.shape, 0)
        c = lax.broadcasted_iota(jnp.int32, ref.shape, 1)
        if ref.shape[0] == LANES:
            c = c % (LANES // 2)
        hit = k == 2 * c if even else k // 2 == c
        ref[...] = jnp.where(hit, 1.0, 0.0).astype(BF16)

    pl.semaphore_wait(barrier, len(around))

    halo = []
    for t in range(tiles):
        lanes = pl.ds(t * LANES, LANES)
        halo.append(send(by_h.at[:, pl.ds(0, 1), lanes], by0.at[:, t, pl.ds(ny, 1)], (0, -1)))
    for t in range(tiles):
        lanes = pl.ds(t * LANES, LANES)
        halo.append(send(bx_h.at[0, :, lanes], bx0.at[nx, t], (-1, 0)))

    for n in range(4, 7 + len(cuts)):
        load(n)

    fill(table_pair, False)
    fill(table_even, True)
    fill(small_pair, False)
    fill(small_even, True)

    def start_rows(p, r, size):
        rows = pl.ds(r, size)
        depth = bz0[p, :, rows, :]
        diag = al0[p, :, rows, :] + bx0[p, :, rows, :] + bx0[p + 1, :, rows, :]
        diag = diag + by0[p, :, rows, :] + by0[p, :, pl.ds(r + 1, size), :]
        diag = diag + depth + z_above(depth)
        inverse = inverse_of(diag)
        diag0[p, :, rows, :] = diag
        inv0[p, :, rows, :] = inverse
        u1[p + 1, :, pl.ds(r + PAD, size), :] = inverse * f0[p, :, rows, :]

    def start_ends(j):
        r = pl.multiple_of(j * 16, 16)
        start_rows(0, r, 16)
        start_rows(nx - 1, r, 16)

    def start_edges(p):
        start_rows(p, 0, 8)
        start_rows(p, ny - 8, 8)

    def start_next(p):
        start_rows(p, edge, edge)
        start_rows(p, ny - 2 * edge, edge)

    def start_inner(p):
        for r in range(2 * edge, ny - 2 * edge, 16):
            start_rows(p, r, 16)

    def send_planes(u):
        rows = pl.ds(PAD, ny)
        return [
            send(u.at[1, :, rows], u.at[nx + 1, :, rows], (-1, 0)),
            send(u.at[nx, :, rows], u.at[0, :, rows], (1, 0)),
        ]

    def send_rows(u):
        planes = pl.ds(1, nx)
        return [
            send(u.at[planes, :, pl.ds(PAD, 1)], u.at[planes, :, pl.ds(PAD + ny, 1)], (0, -1)),
            send(u.at[planes, :, pl.ds(PAD + ny - 1, 1)], u.at[planes, :, pl.ds(PAD - 1, 1)], (0, 1)),
        ]

    def land(copies):
        for copy in copies:
            copy.wait_recv()

    def pair_rows(ref, p, size):
        return ref[p, :, pl.ds(0, size, 2), :] + ref[p, :, pl.ds(1, size, 2), :]

    def restrict_block(level, source, table_p, table_e, plane_list, with_x):
        al, bx, by, bz = source
        al_c, bx_c, by_c, bz_c = coarse[level - 1][:4]
        rows = ny >> level
        more = rows + PAD
        planes = plane_list
        folded = fold_planes([pair_rows(bx, 2 * p, rows) for p in planes], table_p)
        for p, value in zip(planes, folded):
            bx_c[p, :, pl.ds(0, rows), :] = value * 0.0625
        if not with_x:
            return
        folded = fold_planes(
            [by[2 * p, :, pl.ds(0, more, 2), :] + by[2 * p + 1, :, pl.ds(0, more, 2), :] for p in planes], table_p
        )
        for p, value in zip(planes, folded):
            by_c[p, :, pl.ds(0, more), :] = value * 0.0625
        folded = fold_planes([pair_rows(bz, 2 * p, rows) + pair_rows(bz, 2 * p + 1, rows) for p in planes], table_e)
        for p, value in zip(planes, folded):
            bz_c[p, :, pl.ds(0, rows), :] = value * 0.0625
        folded = fold_planes([pair_rows(al, 2 * p, rows) + pair_rows(al, 2 * p + 1, rows) for p in planes], table_p)
        for p, value in zip(planes, folded):
            al_c[p, :, pl.ds(0, rows), :] = value * 0.125

    def coarse_plane(level, p):
        al, bx, by, bz, diag_c, ext = coarse[level - 1][:6]
        _, rows, count = level_dims(dims, level)
        reach = reach_of(dims, level)
        own = pl.ds(0, rows)
        lower_x, lower_y, depth = bx[p, :, own, :], by[p, :, own, :], bz[p, :, own, :]
        diag = al[p, :, own, :] + lower_x + bx[p + 1, :, own, :]
        diag = diag + lower_y + by[p, :, pl.ds(1, rows), :] + depth + z_above(depth)
        diag_c[p, :, :, :] = diag
        place = pl.ds(PAD, rows)
        for a, value in enumerate((lower_x, lower_y, depth, inverse_of(diag))):
            ext[p + reach, pl.ds(a * count, count), place, :] = value

    def send_outer(field, level, ox, oy, part, below=REACH, above=REACH):
        planes, rows, _ = level_dims(dims, level)
        reach = reach_of(dims, level)
        depth = {-1: min(below, reach), 0: planes, 1: min(above, reach)}[ox]
        width = {-1: below, 0: rows, 1: above}[oy]
        from_x = {-1: reach, 0: reach, 1: reach + planes - depth}[ox]
        to_x = {-1: reach + planes, 0: reach, 1: reach - depth}[ox]
        from_y = {-1: PAD, 0: PAD, 1: PAD + rows - width}[oy]
        to_y = {-1: PAD + rows, 0: PAD, 1: PAD - width}[oy]
        return send(
            field.at[pl.ds(from_x, depth), part, pl.ds(from_y, width)],
            field.at[pl.ds(to_x, depth), part, pl.ds(to_y, width)],
            (ox, oy),
        )

    sides = [where for where in around if 0 in where]
    corners = [where for where in around if 0 not in where]

    def send_wide(level, places, arrays, below=REACH, above=REACH - 1):
        count = level_dims(dims, level)[2]
        part = pl.ds(arrays[0] * count, (arrays[1] - arrays[0]) * count)
        return [send_outer(coarse[level - 1][5], level, ox, oy, part, below, above) for ox, oy in places]

    def send_source(level, ox):
        part = pl.ds(0, level_dims(dims, level)[2])
        field = coarse[level - 1][7]
        depth = {-1: REACH - (ox != 0), 0: REACH, 1: REACH - (ox != 0)}
        return [
            send_outer(field, level, ox, oy, part, depth[oy], depth[oy]) for oy in (-1, 1, 0) if (ox, oy) != (0, 0)
        ]

    fine_coeffs = (al0, bx0, by0, bz0)

    def first_coarse(p):
        restrict_block(1, fine_coeffs, table_pair[...], table_even[...], [2 * p, 2 * p + 1], True)

    def first_plane(p):
        coarse_plane(1, p)

    def lower_coarse():
        for level in (2, 3):
            tables = (table_pair, table_even) if level == 2 else (small_pair, small_even)
            planes = nx >> level
            source = coarse[level - 2][:4]
            restrict_block(level, source, tables[0][...], tables[1][...], list(range(planes)), True)
            restrict_block(level, source, tables[0][...], tables[1][...], [planes], False)
            for p in range(planes):
                coarse_plane(level, p)

    def fine_face(ref, size):
        return lambda p, r: ref[p, :, pl.ds(r, size), :]

    def fine_sums(u, p, number, r, size):
        faces = fine_face(bx0, size), fine_face(by0, size), fine_face(bz0, size)
        return neighbour_sums(u, 1, PAD, *faces, p, number, r, size)

    def partial_sum(u, q, r, size):
        rows, here = pl.ds(r, size), pl.ds(r + PAD, size)
        v, depth = u[q + 1, :, here, :], bz0[q, :, rows, :]
        total = depth * z_below(v) + z_above(depth * v)
        ends = isinstance(q, int)
        if not (ends and q == 0):
            total = total + bx0[q, :, rows, :] * u[q, :, here, :]
        if not (ends and q == nx - 1):
            total = total + bx0[q + 1, :, rows, :] * u[q + 2, :, here, :]
        row = lax.broadcasted_iota(jnp.int32, v.shape, 1)
        if r == 0:
            below = jnp.where(row == 0, 0.0, pltpu.roll(v, 1, 1))
        else:
            below = u[q + 1, :, pl.ds(r + PAD - 1, size), :]
        if r + size == ny:
            above = jnp.where(row == size - 1, 0.0, pltpu.roll(v, size - 1, 1))
        else:
            above = u[q + 1, :, pl.ds(r + PAD + 1, size), :]
        return v, total + by0[q, :, rows, :] * below + by0[q, :, pl.ds(r + 1, size), :] * above

    def fine_sweep(weights, fields, target):
        u, older = fields[0], fields[1:]

        def update(p, number, r, size):
            place = pl.ds(r + PAD, size)
            for q, v, total in fine_sums(u, p, number, r, size):
                past = [field[q + 1, :, place, :] for field in older]
                inverse = inv0[q, :, pl.ds(r, size), :]
                target[q + 1, :, place, :] = combine(weights, v, total, inverse, past)

        def partly(q, r, size):
            v, total = partial_sum(u, q, r, size)
            rows, here = pl.ds(r, size), pl.ds(r + PAD, size)
            past = [field[q + 1, :, here, :] for field in older]
            target[q + 1, :, here, :] = combine(weights, v, total, inv0[q, :, rows, :], past)

        def mend(q, rows, face, halo):
            change = inv0[q, :, rows, :] * face * halo
            if weights[1] != 1.0:
                change = change * weights[1]
            here = pl.ds(rows.start + PAD, rows.size)
            target[q + 1, :, here, :] = target[q + 1, :, here, :] + change

        def mend_rows(q):
            for row, face, halo in ((0, 0, PAD - 1), (ny - 1, ny, PAD + ny)):
                mend(q, pl.ds(row, 1), by0[q, :, pl.ds(face, 1), :], u[q + 1, :, pl.ds(halo, 1), :])

        def end_rows(q):
            partly(q, 0, 8)
            partly(q, ny - 8, 8)

        def inner(p, number):
            for r in range(8, ny - 8, 8):
                update(p, number, r, 8)

        def before():
            for r in range(0, ny, 16):
                partly(0, r, 16)
                partly(nx - 1, r, 16)
            loop(1, nx - 1, 4, each(end_rows))

        def outer():
            for r in range(0, ny, 16):
                rows, here = pl.ds(r, 16), pl.ds(r + PAD, 16)
                mend(0, rows, bx0[0, :, rows, :], u[0, :, here, :])
                mend(nx - 1, rows, bx0[nx, :, rows, :], u[nx + 1, :, here, :])
            mend_rows(0)
            mend_rows(nx - 1)
            copies = send_planes(target)
            loop(1, nx - 1, 11, each(mend_rows))
            return copies + send_rows(target)

        def deep(p, number):
            for r in range(16, ny - 16, 8):
                update(p, number, r, 8)

        def shell(p, number):
            update(p, number, 8, 8)
            update(p, number, ny - 16, 8)

        def rest():
            loop(1, nx - 1, 4, shell)
            deep(1, 1)
            deep(nx - 2, 1)

        return before, outer, inner, lambda: loop(2, nx - 2, 4, deep), rest


    sweeps = [fine_sweep(WEIGHTS[k], (u3, u2, u1)[2 - k :], (u2, u3, u4)[k]) for k in range(3)]

    for n in range(4):
        wait_input(n)
    land(halo)
    loop(0, ny // 16, 2, each(start_ends))
    flying = send_planes(u1)
    loop(1, nx - 1, 4, each(start_edges))
    flying += send_rows(u1)
    restrict_block(1, fine_coeffs, table_pair[...], table_even[...], [nx // 2], False)
    for n in range(4, 8):
        wait_input(n)
    loop(1, nx - 1, 4, each(start_next))
    start_inner(1)
    start_inner(nx - 2)
    done = 0
    for g in range(len(cuts) - 1):
        wait_input(8 + g)
        final = g == len(cuts) - 2
        loop(max(cuts[g] - 1, 2), nx - 2 if final else cuts[g + 1] - 1, 2, each(start_inner))
        if g == EARLY - 1:
            sweeps[0][0]()
        if g == EARLY:
            land(flying)
            flying = sweeps[0][1]()
        ready = nx // 4 if final else cuts[g + 1] // 4
        loop(done, ready, 1, each(first_coarse))
        done = ready
    loop(0, nx // 2, 4, each(first_plane))
    wide = send_wide(1, sides, (0, 2))
    loop(1, nx - 1, 4, sweeps[0][2])
    for k in (1, 2):
        sweeps[k][0]()
        land(flying)
        flying = sweeps[k][1]()
        if k == 1:
            wide += send_wide(1, sides, (2, 4), REACH - 1) + send_wide(1, corners, (0, 4), REACH - 1, REACH - 1)
        else:
            for level in (2, 3):
                wide += send_wide(level, sides, (0, 4)) + send_wide(level, corners, (0, 4), REACH - 1, REACH - 1)
        if k == 1:
            loop(1, nx - 1, 4, sweeps[1][2])
            lower_coarse()
            sweeps[2][3]()
        else:
            sweeps[2][4]()

    def residual_rows(p, number, rows):
        for r in rows:
            own = pl.ds(r, 8)
            kept = None
            for q, v, total in fine_sums(u4, 2 * p, 2 * number, r, 8):
                value = f0[q, :, own, :] - diag0[q, :, own, :] * v + total
                if kept is None:
                    kept = q, value
                else:
                    rt[kept[0] // 2, :, own, :] = kept[1] + value
                    kept = None

    def residual_inner(p, number):
        residual_rows(p, number, range(8, ny - 8, 8))

    def residual_partly(p, r, size):
        own = pl.ds(r, size)
        value = 0.0
        for q in (2 * p, 2 * p + 1):
            v, total = partial_sum(u4, q, r, size)
            value = value + (f0[q, :, own, :] - diag0[q, :, own, :] * v + total)
        rt[p, :, own, :] = value

    def residual_edges(p):
        residual_partly(p, 0, 8)
        residual_partly(p, ny - 8, 8)

    def residual_ends():
        for r in range(0, ny, 16):
            residual_partly(0, r, 16)
            residual_partly(nx // 2 - 1, r, 16)

    def residual_mend(p):
        for row, face, halo in ((0, 0, PAD - 1), (ny - 1, ny, PAD + ny)):
            value = rt[p, :, pl.ds(row, 1), :]
            for q in (2 * p, 2 * p + 1):
                value = value + by0[q, :, pl.ds(face, 1), :] * u4[q + 1, :, pl.ds(halo, 1), :]
            rt[p, :, pl.ds(row, 1), :] = value

    def residual_planes():
        for r in range(0, ny, 16):
            own, there = pl.ds(r, 16), pl.ds(r + PAD, 16)
            rt[0, :, own, :] = rt[0, :, own, :] + bx0[0, :, own, :] * u4[0, :, there, :]
            last = nx // 2 - 1
            rt[last, :, own, :] = rt[last, :, own, :] + bx0[nx, :, own, :] * u4[nx + 1, :, there, :]

    loop(1, nx // 2 - 1, 2, residual_inner)
    residual_ends()
    loop(1, nx // 2 - 1, 2, each(residual_edges))
    land(flying)
    residual_planes()
    loop(0, nx // 2, 6, each(residual_mend))

    def put_source(level, p, value):
        _, rows, count = level_dims(dims, level)
        ext, source, first = coarse[level - 1][5:8]
        q = p + reach_of(dims, level)
        own = pl.ds(PAD, rows)
        value = value * 0.125
        if source is not None:
            source[p] = value
        first[q, :, own, :] = ext[q, pl.ds(3 * count, count), own, :] * value

    def first_source(low):
        for first in range(low, low + REACH, 2):
            planes = range(first, first + 2)
            folded = fold_planes([pair_rows(rt, p, ny // 2) for p in planes], table_pair[...])
            for p, value in zip(planes, folded):
                put_source(1, p, value)

    flying = []
    half = nx // 2
    for low_p, ox in ((0, -1), (half - REACH, 1)):
        first_source(low_p)
        flying += send_source(1, ox)
    for low_p in range(REACH, half - REACH, REACH):
        first_source(low_p)
    flying += send_source(1, 0)

    land(wide)
    for level in (1, 2):
        diag_c, ext, source, c1, c2, c3, c4 = coarse[level - 1][4:11]
        fields = [c1, c2, c3, c4]
        planes, rows, count = level_dims(dims, level)
        reach = reach_of(dims, level)
        if level == 1:
            middle = [(reach + 1 + k, reach + planes - 1 - k) for k in range(3)]
            for k, (low_p, high_p) in enumerate(middle):
                first, last = PAD + REACH + k, PAD + rows - REACH - k
                starts = list(range(first, last - 8, 8)) + [last - 8]
                wide_sweep(dims, 1, ext, k, fields, low_p, high_p, [(r, 8) for r in starts], 5)
            land(flying)
            for k, (low_p, high_p) in enumerate(middle):
                full = [(PAD - REACH, 24), (PAD - REACH + 24, rows + 2 * REACH - 24)]
                edges = [(PAD - REACH + k, 8), (PAD + rows - REACH - k, 8)]
                wide_sweep(dims, 1, ext, k, fields, k + 1, low_p, full, 4)
                wide_sweep(dims, 1, ext, k, fields, high_p, planes + 2 * reach - k - 1, full, 4)
                wide_sweep(dims, 1, ext, k, fields, low_p, high_p, edges, 5)
        else:
            land(flying)
            wide_sweeps(dims, level, ext, fields)
        faces = coarse_faces(ext, count, rows)

        def pair(p, number):
            kept = None
            for q, v, total in neighbour_sums(c4, 0, 0, *faces, 2 * p + reach, 2 * number, PAD, rows):
                value = source[q - reach] - diag_c[q - reach] * v + total
                if kept is None:
                    kept = value
                else:
                    c2[(q - reach) // 2, :, pl.ds(0, rows), :] = kept + value
                    kept = None

        loop(0, planes // 2, 3, pair)
        table = table_pair if level == 1 else small_pair
        folded = fold_planes([pair_rows(c2, p, rows // 2) for p in range(planes // 2)], table[...])
        for p, value in enumerate(folded):
            put_source(level + 1, p, value)
        flying = send_source(level + 1, -1) + send_source(level + 1, 1) + send_source(level + 1, 0)
    land(flying)
    for copy in sent:
        copy.wait_send()


def last_kernel(dims, u4, mid, low, ext3, first3, *refs):
    outs, (c2, c3, c4, top, sem) = refs[:4], refs[4:]
    stores = []
    for level, field in enumerate((u4, mid, low)):
        planes, rows, count = level_dims(dims, level)
        own = pl.ds(reach_of(dims, level) if level else 1, planes)
        for t in range(count):
            copy = pltpu.make_async_copy(
                field.at[own, t, pl.ds(PAD, rows)],
                outs[level].at[:, :, pl.ds(t * LANES, LANES)],
                sem.at[len(stores)],
            )
            copy.start()
            stores.append(copy)
    wide_sweeps(dims, 3, ext3, [first3, c2, c3, c4])
    planes, rows, _ = level_dims(dims, 3)
    top[...] = c4[pl.ds(reach_of(dims, 3), planes), 0, pl.ds(PAD, rows), pl.ds(0, LANES // 2)]
    copy = pltpu.make_async_copy(top, outs[3], sem.at[len(stores)])
    copy.start()
    for store in stores + [copy]:
        store.wait()


def space(*shape):
    return pltpu.VMEM(shape, F32)


def halo_shape(dims, level):
    x, y, t = level_dims(dims, level)
    around = reach_of(dims, level) if level else 1
    return (x + 2 * around, t, y + 2 * PAD, LANES)


def scratch_of(dims):
    nx, ny, nz = dims
    tiles = nz // LANES
    shapes = [
        space(nx, tiles, ny, LANES),
        space(nx, tiles, ny, LANES),
        space(nx + 1, tiles, ny, LANES),
        space(nx, tiles, ny + 2 * PAD, LANES),
        space(nx, tiles, ny, LANES),
        space(nx, tiles, ny, LANES),
        space(nx, tiles, ny, LANES),
    ]
    shapes += [space(*halo_shape(dims, 0))] * 3
    shapes += [pltpu.VMEM((2 * LANES, LANES), BF16)] * 2
    shapes += [pltpu.VMEM((LANES, LANES), BF16)] * 2
    for level in (1, 2, 3):
        x, y, t = level_dims(dims, level)
        tall = y + 2 * PAD
        shapes += [
            space(x, t, y, LANES),
            space(x + 1, t, y, LANES),
            space(x, t, tall, LANES),
            space(x, t, y, LANES),
            space(x, t, y, LANES),
        ]
        if level < 3:
            whole = halo_shape(dims, level)
            shapes += [space(whole[0], 4 * t, tall, LANES), space(x, t, y, LANES)]
            shapes += [space(*whole)] * 3
    shapes += [
        pltpu.SemaphoreType.DMA((5, 9 + len(CUTS))),
        pltpu.SemaphoreType.DMA((COPIES,)),
        pltpu.SemaphoreType.DMA((COPIES,)),
    ]
    return shapes


def body(counts, *args):
    dims = args[0].shape
    nx, ny, nz = dims
    whole3 = halo_shape(dims, 3)
    kept = [halo_shape(dims, level) for level in range(3)]
    kept += [(whole3[0], 4) + whole3[2:], whole3]
    in_hbm = pl.BlockSpec(memory_space=pltpu.HBM)
    in_vmem = pl.BlockSpec(memory_space=pltpu.VMEM)
    fields = pl.pallas_call(
        functools.partial(kernel, dims, counts),
        out_shape=[pltpu.VMEM(shape, F32) for shape in kept],
        in_specs=[in_hbm] * 5,
        out_specs=[in_vmem] * 5,
        scratch_shapes=scratch_of(dims),
        compiler_params=pltpu.CompilerParams(
            collective_id=0, has_side_effects=True, vmem_limit_bytes=48 * 2**20
        ),
        name="sweep",
    )(*[pltpu.with_memory_space_constraint(x, pltpu.HBM) for x in args])
    return pl.pallas_call(
        functools.partial(last_kernel, dims),
        out_shape=[pltpu.HBM((nx >> k, ny >> k, nz >> k), F32) for k in range(4)],
        in_specs=[in_vmem] * 5,
        out_specs=[in_hbm] * 4,
        scratch_shapes=[space(*whole3)] * 3
        + [space(nx // 8, ny // 8, LANES // 2), pltpu.SemaphoreType.DMA((16,))],
        compiler_params=pltpu.CompilerParams(vmem_limit_bytes=4 * 2**20),
        name="results",
    )(*[pltpu.with_memory_space_constraint(x, pltpu.VMEM) for x in fields])


def solution(mesh):
    spec = P("gx", "gy", None)
    counts = (mesh.shape["gx"], mesh.shape["gy"])
    return jax.shard_map(
        functools.partial(body, counts),
        mesh=mesh,
        in_specs=(spec,) * 5,
        out_specs=(spec,) * 4,
        check_vma=False,
    )
```
